32 devices in a mesh: face: 4 (over y, x), sub: 8 (over z, core).
Axes of the slice: x: 2, y: 2, z: 4, core: 2. Of those that a mesh axis runs over, the one named last changes fastest.
Arguments:
- field: bfloat16 [3, 4, 32, 32, 256], P(None, 'face', 'sub'), may hold values from -6 to 6
- dw_kernel: float32 [9, 256], replicated, may hold values from -2 to 2
- dw_bias: float32 [256], replicated, may hold values from -3 to 3
- zonal_kernel: float32 [7, 256], replicated, may hold values from -2 to 2
- zonal_bias: float32 [256], replicated, may hold values from -3 to 3
- norm_gain: float32 [256], replicated, may hold values from 0.1 to 1.9
- w_in: bfloat16 [256, 768], replicated, may hold values from -0.375 to 0.375
- w_out: bfloat16 [768, 256], replicated, may hold values from -0.21875 to 0.21875
- layer_scale: float32 [256], replicated, may hold values from 0.5 to 1.5
Outputs:
- output: bfloat16 [3, 4, 32, 32, 256], P(None, 'face', 'sub')
The draws below stay inside these ranges and needn't reach their ends.
All inputs are finite; a program needn't handle non-finite values.
Results may differ from the reference program's by a relative error of at most 0.001.
The reference program's roundings to bfloat16 on the way (of `padded`, `mixed`, `zonal`, `normed` and `hidden`) count: a program that leaves them out, or rounds other values in their place, can miss the bound.
Values may be sent and summed in bfloat16 or wider, within the bound.
No kernel may reach another device: no remote copies, remote signals or barrier semaphores. Data moves between devices by JAX's collectives and lax.ppermute only.
A program may use at most 64 MiB of HBM per device.

```python
import jax
import jax.numpy as jnp
from jax import lax

C = 256
HIDDEN_SIZE = 768
TAPS = 7
DILATION = 4
NSIDE = 32
N_FACE = 4


def block_scale(key, extent, cuts, smallest, high):
    factor_of = 1.0
    for axis_at, blocks in cuts:
        draws = jax.random.uniform(jax.random.fold_in(jax.random.fold_in(key, 6), axis_at), (blocks,), jnp.float32, smallest / len(cuts), high / len(cuts))
        factor_of = factor_of * jnp.repeat(jnp.exp(draws), extent[axis_at] // blocks).reshape((-1,) + (1,) * (len(extent) - 1 - axis_at))
    return factor_of


def gaussian(own_key, dims, width, bound, cuts=(), kind=jnp.bfloat16):
    factor_of = block_scale(own_key, dims, cuts, -0.22, 0.18) if cuts else 1.0
    array = jax.random.normal(own_key, dims, jnp.float32) * width * factor_of
    return jnp.minimum(jnp.maximum(array, -bound), bound).astype(kind)


def setup_inputs(seed: int = 0) -> dict:
    seeds = jax.random.split(jax.random.key(seed), 10)
    field = gaussian(seeds[0], (3, N_FACE, NSIDE, NSIDE, C), 1.0, 6.0, ((1, 4), (2, 8)))
    dw_kernel = gaussian(seeds[1], (9, C), 9 ** -0.5, 2.0, (), jnp.float32)
    dw_bias = gaussian(seeds[2], (C,), 0.5, 3.0, (), jnp.float32)
    zonal_kernel = gaussian(seeds[3], (TAPS, C), TAPS ** -0.5, 2.0, (), jnp.float32)
    zonal_bias = gaussian(seeds[4], (C,), 0.5, 3.0, (), jnp.float32)
    norm_gain = jnp.clip(1.0 + 0.18 * jax.random.normal(seeds[5], (C,), jnp.float32), 0.1, 1.9)
    w_in = gaussian(seeds[6], (C, HIDDEN_SIZE), C ** -0.5, 0.375)
    w_out = gaussian(seeds[7], (HIDDEN_SIZE, C), HIDDEN_SIZE ** -0.5, 0.21875)
    layer_scale = jnp.clip(1.0 + 0.1 * jax.random.normal(seeds[8], (C,), jnp.float32), 0.5, 1.5)
    return dict(field=field, dw_kernel=dw_kernel, dw_bias=dw_bias, zonal_kernel=zonal_kernel, zonal_bias=zonal_bias, norm_gain=norm_gain, w_in=w_in, w_out=w_out, layer_scale=layer_scale)


def cycle_place(facet, column, row_pos, side):
    cycle = (facet + 2) * side - column - row_pos - 1
    along = jnp.where(facet == 0, column + cycle - side, jnp.where((facet == 1) & (cycle < 2 * side), column + cycle - 2 * side, column))
    arc_len = jnp.minimum(jnp.minimum(cycle, side), 4 * side - cycle)
    return (cycle, along, arc_len)

def cycle_cell(cycle, along, side):
    north = (cycle < 2 * side) & (along >= cycle - side)
    middle = jnp.logical_not(north) & (along < 3 * side - cycle)
    facet = jnp.where(north, jnp.int32(0), jnp.where(middle, jnp.int32(1), jnp.int32(2)))
    column = jnp.where(north, along - cycle + side, jnp.where(middle & (cycle < 2 * side), along + 2 * side - cycle, along))
    row_pos = (facet + 2) * side - 1 - cycle - column
    return (facet, column, row_pos)

def pad_face(field, facet, quadrant):
    edge_index = NSIDE - 1
    after = (quadrant + 1) % 4
    before = (quadrant + 3) % 4
    inner = field[facet, quadrant]
    if facet == 0:
        left_col = field[1, quadrant, :, edge_index]
        right_col = field[0, after, edge_index, :]
        top_row = field[1, after, edge_index, :]
        bottom_row = field[0, before, :, edge_index]
    elif facet == 1:
        left_col = field[2, before, :, edge_index]
        right_col = field[0, quadrant, :, 0]
        top_row = field[2, quadrant, edge_index, :]
        bottom_row = field[0, before, 0, :]
    else:
        left_col = field[2, before, 0, :]
        right_col = field[1, after, :, 0]
        top_row = field[2, after, :, 0]
        bottom_row = field[1, quadrant, 0, :]
    corner = jnp.zeros((1, C), field.dtype)
    top_row = jnp.concatenate([corner, top_row, corner], 0)
    bottom_row = jnp.concatenate([corner, bottom_row, corner], 0)
    middle_rows = jnp.concatenate([left_col[:, None], inner, right_col[:, None]], 1)
    return jnp.concatenate([top_row[None], middle_rows, bottom_row[None]], 0)

def reference(field, dw_kernel, dw_bias, zonal_kernel, zonal_bias, norm_gain, w_in, w_out, layer_scale):
    side = NSIDE
    tiles_mixed = []
    for facet in range(3):
        for quadrant in range(4):
            padded = pad_face(field, facet, quadrant).astype(jnp.float32)
            total = jnp.zeros((side, side, C), jnp.float32) + dw_bias
            for i in range(3):
                for j in range(3):
                    total = total + dw_kernel[3 * i + j] * padded[i:i + side, j:j + side]
            tiles_mixed.append(total.astype(jnp.bfloat16))
    mixed = jnp.stack(tiles_mixed).reshape(12 * side * side, C)
    row_pos = lax.broadcasted_iota(jnp.int32, (side, side), 0)
    column = lax.broadcasted_iota(jnp.int32, (side, side), 1)
    half = TAPS // 2
    results = []
    for facet in range(3):
        for quadrant in range(4):
            cycle, along, arc_len = cycle_place(jnp.int32(facet), column, row_pos, side)
            place = quadrant * arc_len + along
            total = jnp.zeros((side * side, C), jnp.float32) + zonal_bias
            for k in range(TAPS):
                moved = (place + DILATION * (k - half)) % (4 * arc_len)
                quad_new = moved // arc_len
                along_new = moved % arc_len
                facet_new, column_new, row_new = cycle_cell(cycle, along_new, side)
                index = ((facet_new * 4 + quad_new) * side + row_new) * side + column_new
                gathered = jnp.take(mixed, index.reshape(-1).astype(jnp.int32), axis=0)
                total = total + zonal_kernel[k] * gathered.astype(jnp.float32)
            zonal = total.astype(jnp.bfloat16)
            values = zonal.astype(jnp.float32)
            mean = lax.optimization_barrier(jnp.mean(values, -1, keepdims=True))
            spread = lax.optimization_barrier(jnp.mean(jnp.square(values - mean), -1, keepdims=True))
            normed = ((values - mean) * lax.rsqrt(spread + 1e-06) * norm_gain).astype(jnp.bfloat16)
            hidden = jax.nn.gelu(jnp.dot(normed, w_in, preferred_element_type=jnp.float32), approximate=False).astype(jnp.bfloat16)
            branch = jnp.dot(hidden, w_out, preferred_element_type=jnp.float32)
            source = field[facet, quadrant].reshape(side * side, C).astype(jnp.float32)
            results.append((source + layer_scale * branch).astype(jnp.bfloat16))
    return jnp.stack(results).reshape(3, 4, side, side, C)
```

```python
import functools

import jax
import jax.numpy as jnp
from jax import lax
from jax.experimental import pallas as pl
from jax.experimental.pallas import tpu as pltpu
from jax.sharding import PartitionSpec as P

TAPS = 7
DILATION = 4
REACH = DILATION * (TAPS // 2)
EPSILON = 1e-06


def fold(count, body, carry, unroll):
    if unroll:
        for i in range(count):
            carry = body(i, carry)
        return carry
    return lax.fori_loop(0, count, body, carry)


def wrap(value, size):
    if isinstance(value, int):
        return value % size
    return lax.rem(value + size, size)


def shift_lanes(values, shift):
    width = values.shape[-1]
    if isinstance(shift, int):
        shift %= width
        if shift == 0:
            return values
    return pltpu.roll(values, shift, values.ndim - 1)


def conv_kernel(quads, subs, side, rows, x_ref, w_ref, o_ref, e_ref, m_ref, ahead_ref, behind_ref):
    width = quads * side
    chans = x_ref.shape[1]
    unroll = width <= 128
    lane = lax.broadcasted_iota(jnp.int32, (chans, width), 1)
    pieces = 3 * rows
    blocks = -(-pieces // quads)

    def load(source):
        return [
            x_ref[source, :, b * width : (b + 1) * width].astype(jnp.float32)
            for b in range(blocks)
        ]

    def to_row(held, face, sub, local):
        piece = face * rows + local
        target = sub * rows + local + (2 - face) * side
        shift = target - (piece % quads) * side
        return shift_lanes(held[piece // quads], wrap(shift, width))

    def plain_row(held, held_before, sub, local):
        y = sub * rows + local
        north = to_row(held, 0, sub, local)
        middle = to_row(held, 1, sub, local)
        south = to_row(held_before, 2, sub, local)
        return jnp.where(lane < y + side, south, jnp.where(lane < y + 2 * side, middle, north))

    last_held = [load(q * subs + subs - 1) for q in range(quads)]
    first_held = [load(q * subs) for q in range(quads)]
    beyond_right, beyond_left = [], []
    for q in range(quads):
        low = plain_row(last_held[q], last_held[q - 1], subs - 1, rows - 1)
        top = plain_row(first_held[q], first_held[q - 1], 0, 0)
        beyond_right.append(shift_lanes(low, 1))
        beyond_left.append(shift_lanes(top, width - 1))

    def build(sub, diagonals):
        diagonals = list(diagonals)
        held = [load(q * subs + sub) for q in range(quads)]
        for q in range(quads):
            for local in range(rows):
                y = sub * rows + local
                row = plain_row(held[q], held[q - 1], sub, local)
                diagonals[2 * q] = jnp.where(lane == y, row, diagonals[2 * q])
                diagonals[2 * q + 1] = jnp.where(
                    lane == y + 3 * side - 1, row, diagonals[2 * q + 1]
                )
                row = jnp.where(lane < y + 3 * side, row, beyond_right[(q + 1) % quads])
                row = jnp.where(lane == wrap(y - 1, width), beyond_left[q - 1], row)
                e_ref[q, side - y] = row
        return tuple(diagonals)

    blank = jnp.zeros((chans, width), jnp.float32)
    diagonals = fold(subs, build, (blank,) * (2 * quads), unroll)
    for q in range(quads):
        after = (q + 1) % quads
        e_ref[q, 0] = jnp.where(
            lane < 3 * side, e_ref[q - 1 if q else quads - 1, side], shift_lanes(diagonals[2 * (q - 1) + 1], 1)
        )
        e_ref[q, side + 1] = jnp.where(
            (lane >= side - 1) & (lane < 3 * side - 1),
            e_ref[after, 1],
            shift_lanes(diagonals[2 * after], width - 1),
        )

    def depthwise(q, u, first=False, last=False):
        below, here, above = e_ref[q, u], e_ref[q, u + 1], e_ref[q, u + 2]
        up_left = shift_lanes(w_ref[0] * above, 2)
        up_right = w_ref[2] * above
        down_left = w_ref[6] * below
        down_right = shift_lanes(w_ref[8] * below, width - 2)
        for k in range(3):
            if first:
                down_left = jnp.where(lane == side - 1 + k * side, 0.0, down_left)
                down_right = jnp.where(lane == 2 * side - 2 + k * side, 0.0, down_right)
            if last:
                up_left = jnp.where(lane == k * side, 0.0, up_left)
                up_right = jnp.where(lane == side - 1 + k * side, 0.0, up_right)
        total = w_ref[9] + w_ref[4] * here
        total = total + (up_right + down_left)
        total = total + shift_lanes(w_ref[1] * above + w_ref[3] * here, 1)
        total = total + shift_lanes(w_ref[5] * here + w_ref[7] * below, width - 1)
        total = total + (up_left + down_right)
        m_ref[q, u] = total.astype(jnp.bfloat16).astype(jnp.float32)

    for q in range(quads):
        depthwise(q, 0, first=True)

        def inner(u, carry, q=q):
            depthwise(q, u + 1)
            return carry

        fold(side - 2, inner, 0, unroll)
        depthwise(q, side - 1, last=True)

    north_cap, south_cap = lane >= 3 * side, lane < side - 1
    arc = jnp.where(north_cap, width - 1 - lane, jnp.where(south_cap, lane + 1, side))
    equator = jnp.logical_not(north_cap | south_cap)
    steps = []
    step = 1
    while step < side:
        steps.insert(0, step)
        step *= 2
    has_step = {step: (arc & step) != 0 for step in steps}

    def sheared(get, head, tail):
        lines = []
        for d in range(side + REACH):
            line = get(0, min(d, side - 1))
            if d < REACH:
                for a in range(1, min(d + 1, REACH)):
                    line = jnp.where(lane == head(a), get(d // a, d % a), line)
            if d >= side:
                for a in range(1, side + REACH - d):
                    place = d - side + a
                    line = jnp.where(
                        lane == tail(a), get(place // a, side - a + place % a), line
                    )
            lines.append(line)
        for step in steps:
            lines = [
                jnp.where(has_step[step], lines[t - step], lines[t]) if t >= step else lines[t]
                for t in range(side + REACH)
            ]
        for t in range(side, side + REACH):
            lines[t] = jnp.where(equator, get(0, t - side), lines[t])
        return lines

    def pole(a):
        return width - 1 - a

    def antipole(a):
        return a - 1

    def extend(q, carry):
        after, before = wrap(q + 1, quads), wrap(q - 1, quads)
        lines = sheared(lambda m, d: m_ref[wrap(after + m, quads), d], pole, antipole)
        for t in range(DILATION, side + REACH):
            if t < side:
                lines[t] = jnp.where(lane >= width - 1 - t, lines[t], m_ref[q, t])
            ahead_ref[q, t - DILATION] = lines[t]
        lines = sheared(
            lambda m, d: m_ref[wrap(before + (-m) % quads, quads), side - 1 - d], antipole, pole
        )
        for t in range(DILATION, side + REACH):
            if t < side:
                lines[t] = jnp.where(lane < t, lines[t], m_ref[q, side - 1 - t])
            behind_ref[q, t - DILATION] = lines[t]
        return carry

    fold(quads, extend, 0, unroll)

    half = TAPS // 2

    def zonal(u, carry):
        for q in range(quads):
            total = w_ref[17] + w_ref[10 + half] * m_ref[q, u]
            for k in range(1, half + 1):
                total = total + w_ref[10 + half + k] * ahead_ref[q, u + DILATION * (k - 1)]
                total = total + w_ref[10 + half - k] * behind_ref[
                    q, side - 1 - u + DILATION * (k - 1)
                ]
            e_ref[q, u] = total
        return carry

    fold(side, zonal, 0, unroll)

    def spread(sub, carry):
        for q in range(quads):
            for b in range(blocks):
                block = None
                for slot in range(quads):
                    piece = b * quads + slot
                    if piece >= pieces:
                        continue
                    face, local = piece // rows, piece % rows
                    y = sub * rows + local
                    strip = q if face < 2 else (q + 1) % quads
                    row = e_ref[strip, side - 1 - y]
                    shift = slot * side - y - (2 - face) * side
                    row = shift_lanes(row, wrap(shift + width, width))
                    block = row if block is None else jnp.where(lane < slot * side, block, row)
                o_ref[q * subs + sub, :, b * width : (b + 1) * width] = block.astype(jnp.bfloat16)
        return carry

    fold(subs, spread, 0, unroll)


def pack_kernel(x_ref, o_ref):
    o_ref[...] = x_ref[...].astype(jnp.float32).T.astype(jnp.bfloat16)


def mlp_kernel(z_ref, x_ref, gain_ref, w_in_ref, w_out_ref, scale_ref, o_ref):
    values = z_ref[...].astype(jnp.float32)
    mean = jnp.mean(values, 0, keepdims=True)
    values = values - mean
    spread = jnp.mean(jnp.square(values), 0, keepdims=True)
    values = values * lax.rsqrt(spread + EPSILON)
    normed = (values.T * gain_ref[...]).astype(jnp.bfloat16)
    inner = jnp.dot(normed, w_in_ref[...], preferred_element_type=jnp.float32)
    hidden = (0.5 * inner * (1.0 + lax.erf(inner * 0.5**0.5))).astype(jnp.bfloat16)
    branch = jnp.dot(hidden, w_out_ref[...], preferred_element_type=jnp.float32)
    o_ref[...] = (x_ref[...].astype(jnp.float32) + scale_ref[...] * branch).astype(jnp.bfloat16)


def shards(
    field, dw_kernel, dw_bias, zonal_kernel, zonal_bias, norm_gain, w_in, w_out, layer_scale
):
    faces, _, rows, side, channels = field.shape
    quads, subs = lax.axis_size("face"), lax.axis_size("sub")
    devices = quads * subs
    share = channels // devices
    cells = faces * rows * side
    width = quads * side
    lanes = -(-cells // width) * width
    chans = -(-share // 8) * 8
    vmem = pl.BlockSpec(memory_space=pltpu.VMEM)
    limit = pltpu.CompilerParams(vmem_limit_bytes=56 * 2**20)

    flat = field.reshape(cells, channels)
    packed = pl.pallas_call(
        pack_kernel,
        out_shape=jax.ShapeDtypeStruct((channels, cells), jnp.bfloat16),
        in_specs=[vmem],
        out_specs=vmem,
        compiler_params=limit,
        name="pack",
    )(flat)
    sent = lax.all_to_all(
        packed.reshape(devices, share, cells), ("face", "sub"), split_axis=0, concat_axis=0, tiled=True
    )
    sent = jnp.pad(sent, ((0, 0), (0, chans - share), (0, lanes - cells)))

    device = lax.axis_index("face") * subs + lax.axis_index("sub")
    weights = jnp.concatenate([dw_kernel, dw_bias[None], zonal_kernel, zonal_bias[None]], 0)
    weights = jnp.pad(weights, ((0, 0), (0, chans - share)))
    weights = lax.dynamic_slice_in_dim(weights, device * share, chans, 1)
    weights = jnp.broadcast_to(weights[:, :, None], weights.shape + (width,))

    extra = side + REACH - DILATION
    zonal = pl.pallas_call(
        functools.partial(conv_kernel, quads, subs, side, rows),
        out_shape=jax.ShapeDtypeStruct((devices, chans, lanes), jnp.bfloat16),
        in_specs=[vmem, vmem],
        out_specs=vmem,
        scratch_shapes=[
            pltpu.VMEM((quads, side + 2, chans, width), jnp.float32),
            pltpu.VMEM((quads, side, chans, width), jnp.float32),
            pltpu.VMEM((quads, extra, chans, width), jnp.float32),
            pltpu.VMEM((quads, extra, chans, width), jnp.float32),
        ],
        compiler_params=limit,
        name="convs",
    )(sent, weights)
    zonal = zonal[:, :share, :cells]
    returned = lax.all_to_all(zonal, ("face", "sub"), split_axis=0, concat_axis=0, tiled=True)

    output = pl.pallas_call(
        mlp_kernel,
        out_shape=jax.ShapeDtypeStruct((cells, channels), jnp.bfloat16),
        in_specs=[vmem] * 6,
        out_specs=vmem,
        compiler_params=limit,
        name="mlp",
    )(returned.reshape(channels, cells), flat, norm_gain[None], w_in, w_out, layer_scale[None])
    return output.reshape(field.shape)


def solution(mesh):
    in_specs = (P(None, "face", "sub", None, None), P(), P(), P(), P(), P(), P(), P(), P())
    out_specs = P(None, "face", "sub", None, None)
    return jax.shard_map(shards, mesh=mesh, in_specs=in_specs, out_specs=out_specs, check_vma=False)
```

```python
import functools

import jax
import jax.numpy as jnp
from jax import lax
from jax.experimental import pallas as pl
from jax.experimental.pallas import tpu as pltpu
from jax.sharding import PartitionSpec as P

TAPS = 7
DILATION = 4
REACH = DILATION * (TAPS // 2)
EPSILON = 1e-06


def fold(count, body, carry, unroll):
    if unroll:
        for i in range(count):
            carry = body(i, carry)
        return carry
    return lax.fori_loop(0, count, body, carry)


def wrap(value, size):
    if isinstance(value, int):
        return value % size
    return lax.rem(value + size, size)


def shift_lanes(values, shift):
    width = values.shape[-1]
    if isinstance(shift, int):
        shift %= width
        if shift == 0:
            return values
    return pltpu.roll(values, shift, values.ndim - 1)


def conv_kernel(quads, subs, side, rows, x_ref, w_ref, o_ref, e_ref, m_ref, ahead_ref, behind_ref):
    width = quads * side
    chans = x_ref.shape[1]
    unroll = width <= 128
    lane = lax.broadcasted_iota(jnp.int32, (chans, width), 1)
    pieces = 3 * rows
    blocks = -(-pieces // quads)

    def load(source):
        return [
            x_ref[source, :, b * width : (b + 1) * width].astype(jnp.float32)
            for b in range(blocks)
        ]

    def to_row(held, face, sub, local):
        piece = face * rows + local
        target = sub * rows + local + (2 - face) * side
        shift = target - (piece % quads) * side
        return shift_lanes(held[piece // quads], wrap(shift, width))

    def plain_row(held, held_before, sub, local):
        y = sub * rows + local
        north = to_row(held, 0, sub, local)
        middle = to_row(held, 1, sub, local)
        south = to_row(held_before, 2, sub, local)
        return jnp.where(lane < y + side, south, jnp.where(lane < y + 2 * side, middle, north))

    last_held = [load(q * subs + subs - 1) for q in range(quads)]
    first_held = [load(q * subs) for q in range(quads)]
    beyond_right, beyond_left = [], []
    for q in range(quads):
        low = plain_row(last_held[q], last_held[q - 1], subs - 1, rows - 1)
        top = plain_row(first_held[q], first_held[q - 1], 0, 0)
        beyond_right.append(shift_lanes(low, 1))
        beyond_left.append(shift_lanes(top, width - 1))

    def build(sub, diagonals):
        diagonals = list(diagonals)
        held = [load(q * subs + sub) for q in range(quads)]
        for q in range(quads):
            for local in range(rows):
                y = sub * rows + local
                row = plain_row(held[q], held[q - 1], sub, local)
                diagonals[2 * q] = jnp.where(lane == y, row, diagonals[2 * q])
                diagonals[2 * q + 1] = jnp.where(
                    lane == y + 3 * side - 1, row, diagonals[2 * q + 1]
                )
                row = jnp.where(lane < y + 3 * side, row, beyond_right[(q + 1) % quads])
                row = jnp.where(lane == wrap(y - 1, width), beyond_left[q - 1], row)
                e_ref[q, side - y] = row
        return tuple(diagonals)

    blank = jnp.zeros((chans, width), jnp.float32)
    diagonals = fold(subs, build, (blank,) * (2 * quads), unroll)
    for q in range(quads):
        after = (q + 1) % quads
        e_ref[q, 0] = jnp.where(
            lane < 3 * side, e_ref[q - 1 if q else quads - 1, side], shift_lanes(diagonals[2 * (q - 1) + 1], 1)
        )
        e_ref[q, side + 1] = jnp.where(
            (lane >= side - 1) & (lane < 3 * side - 1),
            e_ref[after, 1],
            shift_lanes(diagonals[2 * after], width - 1),
        )

    def depthwise(q, u, first=False, last=False):
        below, here, above = e_ref[q, u], e_ref[q, u + 1], e_ref[q, u + 2]
        up_left = shift_lanes(w_ref[0] * above, 2)
        up_right = w_ref[2] * above
        down_left = w_ref[6] * below
        down_right = shift_lanes(w_ref[8] * below, width - 2)
        for k in range(3):
            if first:
                down_left = jnp.where(lane == side - 1 + k * side, 0.0, down_left)
                down_right = jnp.where(lane == 2 * side - 2 + k * side, 0.0, down_right)
            if last:
                up_left = jnp.where(lane == k * side, 0.0, up_left)
                up_right = jnp.where(lane == side - 1 + k * side, 0.0, up_right)
        total = w_ref[9] + w_ref[4] * here
        total = total + (up_right + down_left)
        total = total + shift_lanes(w_ref[1] * above + w_ref[3] * here, 1)
        total = total + shift_lanes(w_ref[5] * here + w_ref[7] * below, width - 1)
        total = total + (up_left + down_right)
        m_ref[q, u] = total.astype(jnp.bfloat16).astype(jnp.float32)

    for q in range(quads):
        depthwise(q, 0, first=True)

        def inner(u, carry, q=q):
            depthwise(q, u + 1)
            return carry

        fold(side - 2, inner, 0, unroll)
        depthwise(q, side - 1, last=True)

    north_cap, south_cap = lane >= 3 * side, lane < side - 1
    arc = jnp.where(north_cap, width - 1 - lane, jnp.where(south_cap, lane + 1, side))
    equator = jnp.logical_not(north_cap | south_cap)
    steps = []
    step = 1
    while step < side:
        steps.insert(0, step)
        step *= 2
    has_step = {step: (arc & step) != 0 for step in steps}

    def sheared(get, head, tail):
        lines = []
        for d in range(side + REACH):
            line = get(0, min(d, side - 1))
            if d < REACH:
                for a in range(1, min(d + 1, REACH)):
                    line = jnp.where(lane == head(a), get(d // a, d % a), line)
            if d >= side:
                for a in range(1, side + REACH - d):
                    place = d - side + a
                    line = jnp.where(
                        lane == tail(a), get(place // a, side - a + place % a), line
                    )
            lines.append(line)
        for step in steps:
            lines = [
                jnp.where(has_step[step], lines[t - step], lines[t]) if t >= step else lines[t]
                for t in range(side + REACH)
            ]
        for t in range(side, side + REACH):
            lines[t] = jnp.where(equator, get(0, t - side), lines[t])
        return lines

    def pole(a):
        return width - 1 - a

    def antipole(a):
        return a - 1

    def extend(q, carry):
        after, before = wrap(q + 1, quads), wrap(q - 1, quads)
        lines = sheared(lambda m, d: m_ref[wrap(after + m, quads), d], pole, antipole)
        for t in range(DILATION, side + REACH):
            if t < side:
                lines[t] = jnp.where(lane >= width - 1 - t, lines[t], m_ref[q, t])
            ahead_ref[q, t - DILATION] = lines[t]
        lines = sheared(
            lambda m, d: m_ref[wrap(before + (-m) % quads, quads), side - 1 - d], antipole, pole
        )
        for t in range(DILATION, side + REACH):
            if t < side:
                lines[t] = jnp.where(lane < t, lines[t], m_ref[q, side - 1 - t])
            behind_ref[q, t - DILATION] = lines[t]
        return carry

    fold(quads, extend, 0, unroll)

    half = TAPS // 2

    def zonal(u, carry):
        for q in range(quads):
            total = w_ref[17] + w_ref[10 + half] * m_ref[q, u]
            for k in range(1, half + 1):
                total = total + w_ref[10 + half + k] * ahead_ref[q, u + DILATION * (k - 1)]
                total = total + w_ref[10 + half - k] * behind_ref[
                    q, side - 1 - u + DILATION * (k - 1)
                ]
            e_ref[q, u] = total
        return carry

    fold(side, zonal, 0, unroll)

    def spread(sub, carry):
        for q in range(quads):
            for b in range(blocks):
                block = None
                for slot in range(quads):
                    piece = b * quads + slot
                    if piece >= pieces:
                        continue
                    face, local = piece // rows, piece % rows
                    y = sub * rows + local
                    strip = q if face < 2 else (q + 1) % quads
                    row = e_ref[strip, side - 1 - y]
                    shift = slot * side - y - (2 - face) * side
                    row = shift_lanes(row, wrap(shift + width, width))
                    block = row if block is None else jnp.where(lane < slot * side, block, row)
                o_ref[q * subs + sub, :, b * width : (b + 1) * width] = block.astype(jnp.bfloat16)
        return carry

    fold(subs, spread, 0, unroll)


def pack_kernel(x_ref, o_ref):
    o_ref[...] = x_ref[...].astype(jnp.float32).T.astype(jnp.bfloat16)


def mlp_kernel(z_ref, x_ref, gain_ref, w_in_ref, w_out_ref, scale_ref, o_ref):
    values = z_ref[...].astype(jnp.float32)
    mean = jnp.mean(values, 0, keepdims=True)
    values = values - mean
    spread = jnp.mean(jnp.square(values), 0, keepdims=True)
    values = values * lax.rsqrt(spread + EPSILON)
    normed = (values.T * gain_ref[...]).astype(jnp.bfloat16)
    inner = jnp.dot(normed, w_in_ref[...], preferred_element_type=jnp.float32)
    hidden = (0.5 * inner * (1.0 + lax.erf(inner * 0.5**0.5))).astype(jnp.bfloat16)
    branch = jnp.dot(hidden, w_out_ref[...], preferred_element_type=jnp.float32)
    o_ref[...] = (x_ref[...].astype(jnp.float32) + scale_ref[...] * branch).astype(jnp.bfloat16)


def shards(
    field, dw_kernel, dw_bias, zonal_kernel, zonal_bias, norm_gain, w_in, w_out, layer_scale
):
    faces, _, rows, side, channels = field.shape
    quads, subs = lax.axis_size("face"), lax.axis_size("sub")
    devices = quads * subs
    share = channels // devices
    cells = faces * rows * side
    width = quads * side
    lanes = -(-cells // width) * width
    chans = -(-share // 8) * 8
    vmem = pl.BlockSpec(memory_space=pltpu.VMEM)
    small = pltpu.CompilerParams(vmem_limit_bytes=2**20 + 24 * cells * channels)
    field_bytes = 4 * devices * chans * lanes
    large = pltpu.CompilerParams(vmem_limit_bytes=2**20 + 7 * field_bytes)

    flat = field.reshape(cells, channels)
    packed = pl.pallas_call(
        pack_kernel,
        out_shape=jax.ShapeDtypeStruct((channels, cells), jnp.bfloat16),
        in_specs=[vmem],
        out_specs=vmem,
        compiler_params=small,
        name="pack",
    )(flat)
    sent = lax.all_to_all(
        packed.reshape(devices, share, cells), ("face", "sub"), split_axis=0, concat_axis=0, tiled=True
    )
    sent = jnp.pad(sent, ((0, 0), (0, chans - share), (0, lanes - cells)))

    device = lax.axis_index("face") * subs + lax.axis_index("sub")
    weights = jnp.concatenate([dw_kernel, dw_bias[None], zonal_kernel, zonal_bias[None]], 0)
    weights = jnp.pad(weights, ((0, 0), (0, chans - share)))
    weights = lax.dynamic_slice_in_dim(weights, device * share, chans, 1)
    weights = jnp.broadcast_to(weights[:, :, None], weights.shape + (width,))

    extra = side + REACH - DILATION
    zonal = pl.pallas_call(
        functools.partial(conv_kernel, quads, subs, side, rows),
        out_shape=jax.ShapeDtypeStruct((devices, chans, lanes), jnp.bfloat16),
        in_specs=[vmem, vmem],
        out_specs=vmem,
        scratch_shapes=[
            pltpu.VMEM((quads, side + 2, chans, width), jnp.float32),
            pltpu.VMEM((quads, side, chans, width), jnp.float32),
            pltpu.VMEM((quads, extra, chans, width), jnp.float32),
            pltpu.VMEM((quads, extra, chans, width), jnp.float32),
        ],
        compiler_params=large,
        name="convs",
    )(sent, weights)
    zonal = zonal[:, :share, :cells]
    returned = lax.all_to_all(zonal, ("face", "sub"), split_axis=0, concat_axis=0, tiled=True)

    output = pl.pallas_call(
        mlp_kernel,
        out_shape=jax.ShapeDtypeStruct((cells, channels), jnp.bfloat16),
        in_specs=[vmem] * 6,
        out_specs=vmem,
        compiler_params=small,
        name="mlp",
    )(returned.reshape(channels, cells), flat, norm_gain[None], w_in, w_out, layer_scale[None])
    return output.reshape(field.shape)


def solution(mesh):
    in_specs = (P(None, "face", "sub", None, None), P(), P(), P(), P(), P(), P(), P(), P())
    out_specs = P(None, "face", "sub", None, None)
    return jax.shard_map(shards, mesh=mesh, in_specs=in_specs, out_specs=out_specs, check_vma=False)
```

```python
import functools

import jax
import jax.numpy as jnp
from jax import lax
from jax.experimental import pallas as pl
from jax.experimental.pallas import tpu as pltpu
from jax.sharding import PartitionSpec as P

TAPS = 7
DILATION = 4
REACH = DILATION * (TAPS // 2)
EPSILON = 1e-06


def fold(count, body, carry, unroll):
    if unroll:
        for i in range(count):
            carry = body(i, carry)
        return carry
    return lax.fori_loop(0, count, body, carry)


def wrap(value, size):
    if isinstance(value, int):
        return value % size
    return lax.rem(value + size, size)


def shift_lanes(values, shift):
    width = values.shape[-1]
    if isinstance(shift, int):
        shift %= width
        if shift == 0:
            return values
    return pltpu.roll(values, shift, values.ndim - 1)


def conv_kernel(quads, subs, side, rows, x_ref, w_ref, o_ref, e_ref, m_ref, ahead_ref, behind_ref):
    width = quads * side
    chans = x_ref.shape[1]
    unroll = width <= 128
    lane = lax.broadcasted_iota(jnp.int32, (chans, width), 1)
    pieces = 3 * rows
    blocks = -(-pieces // quads)

    def load(source):
        return [
            x_ref[source, :, b * width : (b + 1) * width].astype(jnp.float32)
            for b in range(blocks)
        ]

    def to_row(held, face, sub, local):
        piece = face * rows + local
        target = sub * rows + local + (2 - face) * side
        shift = target - (piece % quads) * side
        return shift_lanes(held[piece // quads], wrap(shift, width))

    def plain_row(held, held_before, sub, local):
        y = sub * rows + local
        north = to_row(held, 0, sub, local)
        middle = to_row(held, 1, sub, local)
        south = to_row(held_before, 2, sub, local)
        return jnp.where(lane < y + side, south, jnp.where(lane < y + 2 * side, middle, north))

    last_held = [load(q * subs + subs - 1) for q in range(quads)]
    first_held = [load(q * subs) for q in range(quads)]
    beyond_right, beyond_left = [], []
    for q in range(quads):
        low = plain_row(last_held[q], last_held[q - 1], subs - 1, rows - 1)
        top = plain_row(first_held[q], first_held[q - 1], 0, 0)
        beyond_right.append(shift_lanes(low, 1))
        beyond_left.append(shift_lanes(top, width - 1))

    def build(sub, diagonals):
        diagonals = list(diagonals)
        held = [load(q * subs + sub) for q in range(quads)]
        for q in range(quads):
            for local in range(rows):
                y = sub * rows + local
                row = plain_row(held[q], held[q - 1], sub, local)
                diagonals[2 * q] = jnp.where(lane == y, row, diagonals[2 * q])
                diagonals[2 * q + 1] = jnp.where(
                    lane == y + 3 * side - 1, row, diagonals[2 * q + 1]
                )
                row = jnp.where(lane < y + 3 * side, row, beyond_right[(q + 1) % quads])
                row = jnp.where(lane == wrap(y - 1, width), beyond_left[q - 1], row)
                e_ref[q, side - y] = row
        return tuple(diagonals)

    blank = jnp.zeros((chans, width), jnp.float32)
    diagonals = fold(subs, build, (blank,) * (2 * quads), unroll)
    for q in range(quads):
        after = (q + 1) % quads
        e_ref[q, 0] = jnp.where(
            lane < 3 * side, e_ref[q - 1 if q else quads - 1, side], shift_lanes(diagonals[2 * (q - 1) + 1], 1)
        )
        e_ref[q, side + 1] = jnp.where(
            (lane >= side - 1) & (lane < 3 * side - 1),
            e_ref[after, 1],
            shift_lanes(diagonals[2 * after], width - 1),
        )

    def depthwise(q, u, first=False, last=False):
        below, here, above = e_ref[q, u], e_ref[q, u + 1], e_ref[q, u + 2]
        up_left = shift_lanes(w_ref[0] * above, 2)
        up_right = w_ref[2] * above
        down_left = w_ref[6] * below
        down_right = shift_lanes(w_ref[8] * below, width - 2)
        for k in range(3):
            if first:
                down_left = jnp.where(lane == side - 1 + k * side, 0.0, down_left)
                down_right = jnp.where(lane == 2 * side - 2 + k * side, 0.0, down_right)
            if last:
                up_left = jnp.where(lane == k * side, 0.0, up_left)
                up_right = jnp.where(lane == side - 1 + k * side, 0.0, up_right)
        total = w_ref[9] + w_ref[4] * here
        total = total + (up_right + down_left)
        total = total + shift_lanes(w_ref[1] * above + w_ref[3] * here, 1)
        total = total + shift_lanes(w_ref[5] * here + w_ref[7] * below, width - 1)
        total = total + (up_left + down_right)
        m_ref[q, u] = total.astype(jnp.bfloat16).astype(jnp.float32)

    for q in range(quads):
        depthwise(q, 0, first=True)

        def inner(u, carry, q=q):
            depthwise(q, u + 1)
            return carry

        fold(side - 2, inner, 0, unroll)
        depthwise(q, side - 1, last=True)

    north_cap, south_cap = lane >= 3 * side, lane < side - 1
    arc = jnp.where(north_cap, width - 1 - lane, jnp.where(south_cap, lane + 1, side))
    equator = jnp.logical_not(north_cap | south_cap)
    steps = []
    step = 1
    while step < side:
        steps.insert(0, step)
        step *= 2
    has_step = {step: (arc & step) != 0 for step in steps}

    def sheared(get, head, tail):
        lines = []
        for d in range(side + REACH):
            line = get(0, min(d, side - 1))
            if d < REACH:
                for a in range(1, min(d + 1, REACH)):
                    line = jnp.where(lane == head(a), get(d // a, d % a), line)
            if d >= side:
                for a in range(1, side + REACH - d):
                    place = d - side + a
                    line = jnp.where(
                        lane == tail(a), get(place // a, side - a + place % a), line
                    )
            lines.append(line)
        for step in steps:
            lines = [
                jnp.where(has_step[step], lines[t - step], lines[t]) if t >= step else lines[t]
                for t in range(side + REACH)
            ]
        for t in range(side, side + REACH):
            lines[t] = jnp.where(equator, get(0, t - side), lines[t])
        return lines

    def pole(a):
        return width - 1 - a

    def antipole(a):
        return a - 1

    def extend(q, carry):
        after, before = wrap(q + 1, quads), wrap(q - 1, quads)
        lines = sheared(lambda m, d: m_ref[wrap(after + m, quads), d], pole, antipole)
        for t in range(DILATION, side + REACH):
            if t < side:
                lines[t] = jnp.where(lane >= width - 1 - t, lines[t], m_ref[q, t])
            ahead_ref[q, t - DILATION] = lines[t]
        lines = sheared(
            lambda m, d: m_ref[wrap(before + (-m) % quads, quads), side - 1 - d], antipole, pole
        )
        for t in range(DILATION, side + REACH):
            if t < side:
                lines[t] = jnp.where(lane < t, lines[t], m_ref[q, side - 1 - t])
            behind_ref[q, t - DILATION] = lines[t]
        return carry

    fold(quads, extend, 0, unroll)

    half = TAPS // 2

    def zonal(u, carry):
        for q in range(quads):
            total = w_ref[17] + w_ref[10 + half] * m_ref[q, u]
            for k in range(1, half + 1):
                total = total + w_ref[10 + half + k] * ahead_ref[q, u + DILATION * (k - 1)]
                total = total + w_ref[10 + half - k] * behind_ref[
                    q, side - 1 - u + DILATION * (k - 1)
                ]
            e_ref[q, u] = total
        return carry

    fold(side, zonal, 0, unroll)

    def spread(sub, carry):
        for q in range(quads):
            for b in range(blocks):
                block = None
                for slot in range(quads):
                    piece = b * quads + slot
                    if piece >= pieces:
                        continue
                    face, local = piece // rows, piece % rows
                    y = sub * rows + local
                    strip = q if face < 2 else (q + 1) % quads
                    row = e_ref[strip, side - 1 - y]
                    shift = slot * side - y - (2 - face) * side
                    row = shift_lanes(row, wrap(shift + width, width))
                    block = row if block is None else jnp.where(lane < slot * side, block, row)
                o_ref[q * subs + sub, :, b * width : (b + 1) * width] = block.astype(jnp.bfloat16)
        return carry

    fold(subs, spread, 0, unroll)


def pack_kernel(share, fold_axes, *refs):
    x_hbm, params, o_ref, w_ref, vec_ref = refs[0], refs[1:7], refs[7], refs[8], refs[9]
    x_vmem, held, columns, table, x_sems, sems = refs[10], refs[11:17], refs[17], refs[18], refs[19], refs[20]
    parts = x_vmem.shape[0]
    rows = x_vmem.shape[1]
    loads = [
        pltpu.make_async_copy(x_hbm.at[pl.ds(i * rows, rows)], x_vmem.at[i], x_sems.at[i])
        for i in range(parts)
    ]
    small = [
        pltpu.make_async_copy(source, target, sems.at[i])
        for i, (source, target) in enumerate(zip(params, held, strict=True))
    ]
    for copy in small + loads:
        copy.start()
    for copy in small:
        copy.wait()
    first = 0
    for target in held[:4]:
        table[first : first + target.shape[0], :] = target[...]
        first += target.shape[0]
    vec_ref[0:1, :] = held[4][...]
    vec_ref[1:2, :] = held[5][...]
    channels = table.shape[1]
    columns[0:channels, :] = table[...].T
    device = lax.axis_index(fold_axes[0]) * lax.axis_size(fold_axes[1]) + lax.axis_index(fold_axes[1])
    start = device * share
    if share % 8 == 0:
        start = pl.multiple_of(start, 8)
    mine = columns[pl.ds(start, w_ref.shape[1]), :]
    for k in range(w_ref.shape[0]):
        w_ref[k] = jnp.broadcast_to(mine[:, k : k + 1], w_ref.shape[1:])
    for i in range(parts):
        loads[i].wait()
        o_ref[:, i * rows : (i + 1) * rows] = (
            x_vmem[i].astype(jnp.float32).T.astype(jnp.bfloat16)
        )


def mlp_kernel(z_ref, x_ref, vec_ref, w_in_ref, w_out_ref, o_hbm, o_vmem, sems):
    parts, rows = o_vmem.shape[0], o_vmem.shape[1]
    gain, scale = vec_ref[0:1, :], vec_ref[1:2, :]
    stores = []
    for i in range(parts):
        values = z_ref[:, i * rows : (i + 1) * rows].astype(jnp.float32)
        mean = jnp.mean(values, 0, keepdims=True)
        values = values - mean
        spread = jnp.mean(jnp.square(values), 0, keepdims=True)
        values = values * lax.rsqrt(spread + EPSILON)
        normed = (values.T * gain).astype(jnp.bfloat16)
        inner = jnp.dot(normed, w_in_ref[...], preferred_element_type=jnp.float32)
        hidden = (0.5 * inner * (1.0 + lax.erf(inner * 0.5**0.5))).astype(jnp.bfloat16)
        branch = jnp.dot(hidden, w_out_ref[...], preferred_element_type=jnp.float32)
        source = x_ref[i * rows : (i + 1) * rows, :].astype(jnp.float32)
        o_vmem[i] = (source + scale * branch).astype(jnp.bfloat16)
        store = pltpu.make_async_copy(o_vmem.at[i], o_hbm.at[pl.ds(i * rows, rows)], sems.at[i])
        store.start()
        stores.append(store)
    for store in stores:
        store.wait()


def shards(
    field, dw_kernel, dw_bias, zonal_kernel, zonal_bias, norm_gain, w_in, w_out, layer_scale
):
    faces, _, rows, side, channels = field.shape
    quads, subs = lax.axis_size("face"), lax.axis_size("sub")
    devices = quads * subs
    share = channels // devices
    cells = faces * rows * side
    width = quads * side
    lanes = -(-cells // width) * width
    chans = -(-share // 8) * 8
    vmem = pl.BlockSpec(memory_space=pltpu.VMEM)
    small = pltpu.CompilerParams(vmem_limit_bytes=2**20 + 24 * cells * channels)
    field_bytes = 4 * devices * chans * lanes
    large = pltpu.CompilerParams(vmem_limit_bytes=2**20 + 7 * field_bytes)

    flat = field.reshape(cells, channels)
    hbm = pl.BlockSpec(memory_space=pltpu.HBM)
    part = 128
    parts = cells // part
    params = (
        dw_kernel, dw_bias[None], zonal_kernel, zonal_bias[None], norm_gain[None], layer_scale[None]
    )
    taps = sum(p.shape[0] for p in params[:4])
    packed, weights, vectors = pl.pallas_call(
        functools.partial(pack_kernel, share, ("face", "sub")),
        out_shape=(
            jax.ShapeDtypeStruct((channels, cells), jnp.bfloat16),
            jax.ShapeDtypeStruct((taps, chans, width), jnp.float32),
            jax.ShapeDtypeStruct((2, channels), jnp.float32),
        ),
        in_specs=[hbm] * 7,
        out_specs=(vmem, vmem, vmem),
        scratch_shapes=[pltpu.VMEM((parts, part, channels), jnp.bfloat16)]
        + [pltpu.VMEM(p.shape, jnp.float32) for p in params]
        + [
            pltpu.VMEM((channels + chans, 128), jnp.float32),
            pltpu.VMEM((128, channels), jnp.float32),
            pltpu.SemaphoreType.DMA((parts,)),
            pltpu.SemaphoreType.DMA((len(params),)),
        ],
        compiler_params=small,
        name="pack",
    )(*(pltpu.with_memory_space_constraint(array, pltpu.HBM) for array in (flat, *params)))
    sent = lax.all_to_all(
        packed.reshape(devices, share, cells), ("face", "sub"), split_axis=0, concat_axis=0, tiled=True
    )
    sent = jnp.pad(sent, ((0, 0), (0, chans - share), (0, lanes - cells)))

    extra = side + REACH - DILATION
    zonal = pl.pallas_call(
        functools.partial(conv_kernel, quads, subs, side, rows),
        out_shape=jax.ShapeDtypeStruct((devices, chans, lanes), jnp.bfloat16),
        in_specs=[vmem, vmem],
        out_specs=vmem,
        scratch_shapes=[
            pltpu.VMEM((quads, side + 2, chans, width), jnp.float32),
            pltpu.VMEM((quads, side, chans, width), jnp.float32),
            pltpu.VMEM((quads, extra, chans, width), jnp.float32),
            pltpu.VMEM((quads, extra, chans, width), jnp.float32),
        ],
        compiler_params=large,
        name="convs",
    )(sent, weights)
    zonal = zonal[:, :share, :cells]
    returned = lax.all_to_all(zonal, ("face", "sub"), split_axis=0, concat_axis=0, tiled=True)

    output = pl.pallas_call(
        mlp_kernel,
        out_shape=jax.ShapeDtypeStruct((cells, channels), jnp.bfloat16),
        in_specs=[vmem] * 5,
        out_specs=hbm,
        scratch_shapes=[
            pltpu.VMEM((parts, part, channels), jnp.bfloat16),
            pltpu.SemaphoreType.DMA((parts,)),
        ],
        compiler_params=small,
        name="mlp",
    )(returned.reshape(channels, cells), flat, vectors, w_in, w_out)
    return output.reshape(field.shape)


def solution(mesh):
    in_specs = (P(None, "face", "sub", None, None), P(), P(), P(), P(), P(), P(), P(), P())
    out_specs = P(None, "face", "sub", None, None)
    return jax.shard_map(shards, mesh=mesh, in_specs=in_specs, out_specs=out_specs, check_vma=False)
```

```python
import functools

import jax
import jax.numpy as jnp
from jax import lax
from jax.experimental import pallas as pl
from jax.experimental.pallas import tpu as pltpu
from jax.sharding import PartitionSpec as P

TAPS = 7
DILATION = 4
REACH = DILATION * (TAPS // 2)
EPSILON = 1e-06


def fold(count, body, carry, unroll):
    if unroll:
        for i in range(count):
            carry = body(i, carry)
        return carry
    return lax.fori_loop(0, count, body, carry)


def wrap(value, size):
    if isinstance(value, int):
        return value % size
    return lax.rem(value + size, size)


def shift_lanes(values, shift):
    width = values.shape[-1]
    if isinstance(shift, int):
        shift %= width
        if shift == 0:
            return values
    return pltpu.roll(values, shift, values.ndim - 1)


def piece_at(block, slot, faces=3):
    group, at = divmod(block, faces)
    first = group * (faces + 1)
    if slot < faces:
        return faces - 1 - slot, first + at
    return faces - 1 - at, first + faces


def conv_kernel(
    quads, subs, side, rows, x_ref, w_ref, o_ref, e_ref, m_ref, ahead_ref, behind_ref, head_ref, tail_ref
):
    width = quads * side
    chans = x_ref.shape[1]
    unroll = width <= 128
    lane = lax.broadcasted_iota(jnp.int32, (chans, width), 1)
    blocks = 3 * rows // quads

    def load(source):
        return [
            x_ref[source, :, b * width : (b + 1) * width].astype(jnp.float32)
            for b in range(blocks)
        ]

    def plain_row(held, held_before, sub, local):
        group, at = divmod(local, 4)
        y = sub * rows + local
        first = 3 * group
        if at < 3:
            row = jnp.where(lane < side, held_before[first + at], held[first + at])
            return shift_lanes(row, y)
        south = shift_lanes(held_before[first], wrap(y - 3 * side, width))
        middle = shift_lanes(held[first + 1], wrap(y - 2 * side, width))
        north = shift_lanes(held[first + 2], wrap(y - side, width))
        return jnp.where(lane < y + side, south, jnp.where(lane < y + 2 * side, middle, north))

    last_held = [load(q * subs + subs - 1) for q in range(quads)]
    first_held = [load(q * subs) for q in range(quads)]
    beyond_right, beyond_left = [], []
    for q in range(quads):
        low = plain_row(last_held[q], last_held[q - 1], subs - 1, rows - 1)
        top = plain_row(first_held[q], first_held[q - 1], 0, 0)
        beyond_right.append(shift_lanes(low, 1))
        beyond_left.append(shift_lanes(top, width - 1))

    def build(sub, diagonals):
        diagonals = list(diagonals)
        held = [load(q * subs + sub) for q in range(quads)]
        for q in range(quads):
            for local in range(rows):
                y = sub * rows + local
                row = plain_row(held[q], held[q - 1], sub, local)
                diagonals[2 * q] = jnp.where(lane == y, row, diagonals[2 * q])
                diagonals[2 * q + 1] = jnp.where(
                    lane == y + 3 * side - 1, row, diagonals[2 * q + 1]
                )
                row = jnp.where(lane < y + 3 * side, row, beyond_right[(q + 1) % quads])
                row = jnp.where(lane == wrap(y - 1, width), beyond_left[q - 1], row)
                e_ref[q, side - y] = row
        return tuple(diagonals)

    blank = jnp.zeros((chans, width), jnp.float32)
    diagonals = fold(subs, build, (blank,) * (2 * quads), unroll)
    for q in range(quads):
        after = (q + 1) % quads
        before = (q - 1) % quads
        e_ref[q, 0] = jnp.where(
            lane < 3 * side, e_ref[before, side], shift_lanes(diagonals[2 * before + 1], 1)
        )
        e_ref[q, side + 1] = jnp.where(
            (lane >= side - 1) & (lane < 3 * side - 1),
            e_ref[after, 1],
            shift_lanes(diagonals[2 * after], width - 1),
        )

    def depthwise(q, u, first=False, last=False):
        below, here, above = e_ref[q, u], e_ref[q, u + 1], e_ref[q, u + 2]
        up_left = shift_lanes(w_ref[0] * above, 2)
        up_right = w_ref[2] * above
        down_left = w_ref[6] * below
        down_right = shift_lanes(w_ref[8] * below, width - 2)
        for k in range(3):
            if first:
                down_left = jnp.where(lane == side - 1 + k * side, 0.0, down_left)
                down_right = jnp.where(lane == 2 * side - 2 + k * side, 0.0, down_right)
            if last:
                up_left = jnp.where(lane == k * side, 0.0, up_left)
                up_right = jnp.where(lane == side - 1 + k * side, 0.0, up_right)
        total = w_ref[9] + w_ref[4] * here
        total = total + (up_right + down_left)
        total = total + shift_lanes(w_ref[1] * above + w_ref[3] * here, 1)
        total = total + shift_lanes(w_ref[5] * here + w_ref[7] * below, width - 1)
        total = total + (up_left + down_right)
        m_ref[q, u] = total.astype(jnp.bfloat16).astype(jnp.float32)

    for q in range(quads):
        depthwise(q, 0, first=True)

        def inner(u, carry, q=q):
            depthwise(q, u + 1)
            return carry

        fold(side - 2, inner, 0, unroll)
        depthwise(q, side - 1, last=True)

    north_cap, south_cap = lane >= 3 * side, lane < side - 1
    northern = lane >= 2 * side
    arc = jnp.where(north_cap, width - 1 - lane, jnp.where(south_cap, lane + 1, side))
    equator = jnp.logical_not(north_cap | south_cap)
    steps = []
    step = 1
    while step < side:
        steps.append(step)
        step *= 2
    has_step = {step: (arc & step) != 0 for step in steps}
    for j in range(quads):
        back = (quads - j) % quads
        for d in range(REACH):
            head_ref[j, d] = jnp.where(northern, m_ref[j, d], m_ref[back, side - 1 - d])

        def join(d, carry, j=j, back=back):
            tail_ref[j, d] = jnp.where(northern, m_ref[back, side - 1 - d], m_ref[j, d])
            return carry

        fold(side, join, 0, unroll)

    def sheared(inputs):
        seen = {}

        def line(level, t):
            if level == len(steps):
                return inputs.get(t)
            if (level, t) not in seen:
                step = steps[level]
                still, moved = line(level + 1, t), line(level + 1, t - step)
                if still is not None and moved is not None:
                    moved = jnp.where(has_step[step], moved, still)
                seen[level, t] = still if moved is None else moved
            return seen[level, t]

        return lambda t: line(0, t)

    def extend(j, carry):
        back = wrap(quads - j, quads)
        forth_strip, back_strip = wrap(j - 1, quads), wrap(quads + 1 - j, quads)
        heads, tails = {}, {}
        for d in range(REACH):
            line = head_ref[j, d]
            for a in range(1, min(d + 1, REACH)):
                line = jnp.where(arc == a, head_ref[wrap(j + d // a, quads), d % a], line)
            heads[d] = line
        for d in range(1, side):
            tails[d] = tail_ref[j, d]
        for d in range(side, side + REACH - 1):
            line = None
            for a in range(1, side + REACH - d):
                place = d - side + a
                moved = tail_ref[wrap(j + place // a, quads), side - a + place % a]
                line = moved if line is None else jnp.where(arc == a, moved, line)
            tails[d] = line
        head, tail = sheared(heads), sheared(tails)
        for t in range(DILATION, side + REACH):
            line = head(t)
            if t < side:
                ahead = jnp.where(lane >= width - 1 - t, line, m_ref[forth_strip, t])
                behind = jnp.where(lane < t, line, m_ref[back_strip, side - 1 - t])
            else:
                end = tail(t)
                ahead = jnp.where(south_cap, end, end if line is None else line)
                behind = jnp.where(north_cap, end, end if line is None else line)
                ahead = jnp.where(equator, m_ref[j, t - side], ahead)
                behind = jnp.where(equator, m_ref[back, 2 * side - 1 - t], behind)
            ahead_ref[forth_strip, t - DILATION] = ahead
            behind_ref[back_strip, t - DILATION] = behind
        return carry

    fold(quads, extend, 0, unroll)

    half = TAPS // 2

    def zonal(u, carry):
        for q in range(quads):
            total = w_ref[17] + w_ref[10 + half] * m_ref[q, u]
            for k in range(1, half + 1):
                total = total + w_ref[10 + half + k] * ahead_ref[q, u + DILATION * (k - 1)]
                total = total + w_ref[10 + half - k] * behind_ref[
                    q, side - 1 - u + DILATION * (k - 1)
                ]
            e_ref[q, u] = total
        return carry

    fold(side, zonal, 0, unroll)

    def spread(sub, carry):
        def row(q, local):
            return e_ref[q % quads, side - 1 - sub * rows - local]

        for group in range(rows // 4):
            first = 4 * group
            y = sub * rows + first
            aligned = [
                [shift_lanes(row(q, first + at), wrap(width - y - at, width)) for q in range(quads)]
                for at in range(3)
            ]
            for q in range(quads):
                for at in range(3):
                    rest = row(q + 1 if at == 0 else q, first + 3)
                    rest = shift_lanes(rest, wrap((3 - at) * side - y - 3 + width, width))
                    block = jnp.where(
                        lane < side,
                        aligned[at][(q + 1) % quads],
                        jnp.where(lane < 3 * side, aligned[at][q], rest),
                    )
                    b = 3 * group + at
                    o_ref[q * subs + sub, :, b * width : (b + 1) * width] = block.astype(
                        jnp.bfloat16
                    )
        return carry

    fold(subs, spread, 0, unroll)


def pack_kernel(share, fold_axes, *refs):
    x_hbm, params, o_ref, w_ref, vec_ref = refs[0], refs[1:7], refs[7], refs[8], refs[9]
    x_vmem, held, columns, table, x_sems, sems = refs[10], refs[11:17], refs[17], refs[18], refs[19], refs[20]
    rows, _, side, channels = x_vmem.shape
    order = [at for at in range(rows) if at % 4 == 3] + [at for at in range(rows) if at % 4 != 3]
    loads = [
        pltpu.make_async_copy(x_hbm.at[:, at], x_vmem.at[at], x_sems.at[at]) for at in order
    ]
    small = [
        pltpu.make_async_copy(source, target, sems.at[i])
        for i, (source, target) in enumerate(zip(params, held, strict=True))
    ]
    for copy in small + loads:
        copy.start()
    for copy in small:
        copy.wait()
    first = 0
    for target in held[:4]:
        table[first : first + target.shape[0], :] = target[...]
        first += target.shape[0]
    vec_ref[0:1, :] = held[4][...]
    vec_ref[1:2, :] = held[5][...]
    columns[0:channels, :] = table[...].T
    device = lax.axis_index(fold_axes[0]) * lax.axis_size(fold_axes[1]) + lax.axis_index(fold_axes[1])
    start = device * share
    if share % 8 == 0:
        start = pl.multiple_of(start, 8)
    mine = columns[pl.ds(start, w_ref.shape[1]), :]
    for k in range(w_ref.shape[0]):
        w_ref[k] = jnp.broadcast_to(mine[:, k : k + 1], w_ref.shape[1:])
    width = 4 * side
    for block in range(3 * rows // 4):
        if block % 3 == 0:
            loads[block // 3].wait()
        loads[rows // 4 + block].wait()
        pieces = [x_vmem[local, face] for face, local in (piece_at(block, k) for k in range(4))]
        o_ref[:, block * width : (block + 1) * width] = jnp.concatenate(pieces, 0).T


def mlp_kernel(z_ref, x_ref, vec_ref, w_in_ref, w_out_ref, o_hbm, o_vmem, sems):
    parts, slots, side, _ = o_vmem.shape
    width = slots * side
    gain, scale = vec_ref[0:1, :], vec_ref[1:2, :]
    stores = []
    for i in range(parts):
        values = z_ref[:, i * width : (i + 1) * width].astype(jnp.float32)
        mean = jnp.mean(values, 0, keepdims=True)
        values = values - mean
        spread = jnp.mean(jnp.square(values), 0, keepdims=True)
        values = values * lax.rsqrt(spread + EPSILON)
        normed = (values.T * gain).astype(jnp.bfloat16)
        inner = jnp.dot(normed, w_in_ref[...], preferred_element_type=jnp.float32)
        hidden = (0.5 * inner * (1.0 + lax.erf(inner * 0.5**0.5))).astype(jnp.bfloat16)
        branch = jnp.dot(hidden, w_out_ref[...], preferred_element_type=jnp.float32)
        for k in range(slots):
            face, local = piece_at(i, k)
            source = x_ref[face, local].astype(jnp.float32)
            place = face if k < slots - 1 else k
            o_vmem[i, place] = (source + scale * branch[k * side : (k + 1) * side]).astype(jnp.bfloat16)
        line = piece_at(i, 0)[1]
        face, local = piece_at(i, slots - 1)
        for at, (source, target) in enumerate(
            (
                (o_vmem.at[i, pl.ds(0, slots - 1)], o_hbm.at[:, line]),
                (o_vmem.at[i, slots - 1], o_hbm.at[face, local]),
            )
        ):
            store = pltpu.make_async_copy(source, target, sems.at[2 * i + at])
            store.start()
            stores.append(store)
    for store in stores:
        store.wait()


def shards(
    field, dw_kernel, dw_bias, zonal_kernel, zonal_bias, norm_gain, w_in, w_out, layer_scale
):
    faces, _, rows, side, channels = field.shape
    quads, subs = lax.axis_size("face"), lax.axis_size("sub")
    devices = quads * subs
    share = channels // devices
    cells = faces * rows * side
    width = quads * side
    lanes = -(-cells // width) * width
    chans = -(-share // 8) * 8
    vmem = pl.BlockSpec(memory_space=pltpu.VMEM)
    small = pltpu.CompilerParams(vmem_limit_bytes=2**20 + 24 * cells * channels)
    field_bytes = 4 * devices * chans * lanes
    large = pltpu.CompilerParams(vmem_limit_bytes=2**20 + 9 * field_bytes)

    local = field.reshape(faces, rows, side, channels)
    hbm = pl.BlockSpec(memory_space=pltpu.HBM)
    params = (
        dw_kernel, dw_bias[None], zonal_kernel, zonal_bias[None], norm_gain[None], layer_scale[None]
    )
    taps = sum(p.shape[0] for p in params[:4])
    packed, weights, vectors = pl.pallas_call(
        functools.partial(pack_kernel, share, ("face", "sub")),
        out_shape=(
            jax.ShapeDtypeStruct((channels, cells), jnp.bfloat16),
            jax.ShapeDtypeStruct((taps, chans, width), jnp.float32),
            jax.ShapeDtypeStruct((2, channels), jnp.float32),
        ),
        in_specs=[hbm] * 7,
        out_specs=(vmem, vmem, vmem),
        scratch_shapes=[pltpu.VMEM((rows, faces, side, channels), jnp.bfloat16)]
        + [pltpu.VMEM(p.shape, jnp.float32) for p in params]
        + [
            pltpu.VMEM((channels + chans, 128), jnp.float32),
            pltpu.VMEM((128, channels), jnp.float32),
            pltpu.SemaphoreType.DMA((rows,)),
            pltpu.SemaphoreType.DMA((len(params),)),
        ],
        compiler_params=small,
        name="pack",
    )(*(pltpu.with_memory_space_constraint(array, pltpu.HBM) for array in (local, *params)))
    sent = lax.all_to_all(
        packed.reshape(devices, share, cells), ("face", "sub"), split_axis=0, concat_axis=0, tiled=True
    )
    sent = jnp.pad(sent, ((0, 0), (0, chans - share), (0, lanes - cells)))

    extra = side + REACH - DILATION
    zonal = pl.pallas_call(
        functools.partial(conv_kernel, quads, subs, side, rows),
        out_shape=jax.ShapeDtypeStruct((devices, chans, lanes), jnp.bfloat16),
        in_specs=[vmem, vmem],
        out_specs=vmem,
        scratch_shapes=[
            pltpu.VMEM((quads, side + 2, chans, width), jnp.float32),
            pltpu.VMEM((quads, side, chans, width), jnp.float32),
            pltpu.VMEM((quads, extra, chans, width), jnp.float32),
            pltpu.VMEM((quads, extra, chans, width), jnp.float32),
            pltpu.VMEM((quads, REACH, chans, width), jnp.float32),
            pltpu.VMEM((quads, side, chans, width), jnp.float32),
        ],
        compiler_params=large,
        name="convs",
    )(sent, weights)
    zonal = zonal[:, :share, :cells]
    returned = lax.all_to_all(zonal, ("face", "sub"), split_axis=0, concat_axis=0, tiled=True)

    output = pl.pallas_call(
        mlp_kernel,
        out_shape=jax.ShapeDtypeStruct(local.shape, jnp.bfloat16),
        in_specs=[vmem] * 5,
        out_specs=hbm,
        scratch_shapes=[
            pltpu.VMEM((cells // width, quads, side, channels), jnp.bfloat16),
            pltpu.SemaphoreType.DMA((2 * cells // width,)),
        ],
        compiler_params=small,
        name="mlp",
    )(returned.reshape(channels, cells), local, vectors, w_in, w_out)
    return output.reshape(field.shape)


def solution(mesh):
    in_specs = (P(None, "face", "sub", None, None), P(), P(), P(), P(), P(), P(), P(), P())
    out_specs = P(None, "face", "sub", None, None)
    return jax.shard_map(shards, mesh=mesh, in_specs=in_specs, out_specs=out_specs, check_vma=False)
```

```python
import functools

import jax
import jax.numpy as jnp
from jax import lax
from jax.experimental import pallas as pl
from jax.experimental.pallas import tpu as pltpu
from jax.sharding import PartitionSpec as P

TAPS = 7
DILATION = 4
REACH = DILATION * (TAPS // 2)
EPSILON = 1e-06


def fold(count, body, carry, unroll):
    if unroll:
        for i in range(count):
            carry = body(i, carry)
        return carry
    return lax.fori_loop(0, count, body, carry)


def wrap(value, size):
    if isinstance(value, int):
        return value % size
    return lax.rem(value + size, size)


def shift_lanes(values, shift):
    width = values.shape[-1]
    if isinstance(shift, int):
        shift %= width
        if shift == 0:
            return values
    return pltpu.roll(values, shift, values.ndim - 1)


def piece_at(block, slot, faces=3):
    group, at = divmod(block, faces)
    first = group * (faces + 1)
    if slot < faces:
        return faces - 1 - slot, first + at
    return faces - 1 - at, first + faces


def conv_kernel(
    quads, subs, side, rows, share, axes, x_ref, dw_ref, dw_bias_ref, zonal_ref, zonal_bias_ref, o_ref,
    e_ref, m_ref, ahead_ref, behind_ref, head_ref, tail_ref, columns, table, w_ref
):
    lay_out(share, axes, (dw_ref, dw_bias_ref, zonal_ref, zonal_bias_ref), columns, table, w_ref)
    width = quads * side
    chans = x_ref.shape[1]
    unroll = width <= 128
    lane = lax.broadcasted_iota(jnp.int32, (chans, width), 1)
    blocks = 3 * rows // quads

    def load(source):
        return [
            x_ref[source, :, b * width : (b + 1) * width].astype(jnp.float32)
            for b in range(blocks)
        ]

    def plain_row(held, held_before, sub, local):
        group, at = divmod(local, 4)
        y = sub * rows + local
        first = 3 * group
        if at < 3:
            row = jnp.where(lane < side, held_before[first + at], held[first + at])
            return shift_lanes(row, y)
        south = shift_lanes(held_before[first], wrap(y - 3 * side, width))
        middle = shift_lanes(held[first + 1], wrap(y - 2 * side, width))
        north = shift_lanes(held[first + 2], wrap(y - side, width))
        return jnp.where(lane < y + side, south, jnp.where(lane < y + 2 * side, middle, north))

    last_held = [load(q * subs + subs - 1) for q in range(quads)]
    first_held = [load(q * subs) for q in range(quads)]
    beyond_right, beyond_left = [], []
    for q in range(quads):
        low = plain_row(last_held[q], last_held[q - 1], subs - 1, rows - 1)
        top = plain_row(first_held[q], first_held[q - 1], 0, 0)
        beyond_right.append(shift_lanes(low, 1))
        beyond_left.append(shift_lanes(top, width - 1))

    def build(sub, diagonals):
        diagonals = list(diagonals)
        held = [load(q * subs + sub) for q in range(quads)]
        for q in range(quads):
            for local in range(rows):
                y = sub * rows + local
                row = plain_row(held[q], held[q - 1], sub, local)
                diagonals[2 * q] = jnp.where(lane < y, diagonals[2 * q], row)
                diagonals[2 * q + 1] = jnp.where(
                    lane < y + 3 * side - 1, diagonals[2 * q + 1], row
                )
                row = jnp.where(lane < y + 3 * side, row, beyond_right[(q + 1) % quads])
                row = jnp.where(lane == wrap(y - 1, width), beyond_left[q - 1], row) if not isinstance(y, int) or y == 0 else jnp.where(lane < y, beyond_left[q - 1], row)
                e_ref[q, side - y] = row
        return tuple(diagonals)

    blank = jnp.zeros((chans, width), jnp.float32)
    diagonals = fold(subs, build, (blank,) * (2 * quads), unroll)
    for q in range(quads):
        after = (q + 1) % quads
        before = (q - 1) % quads
        e_ref[q, 0] = jnp.where(
            lane < 3 * side, e_ref[before, side], shift_lanes(diagonals[2 * before + 1], 1)
        )
        e_ref[q, side + 1] = jnp.where(
            (lane >= side - 1) & (lane < 3 * side - 1),
            e_ref[after, 1],
            shift_lanes(diagonals[2 * after], width - 1),
        )

    def depthwise(q, u, first=False, last=False):
        below, here, above = e_ref[q, u], e_ref[q, u + 1], e_ref[q, u + 2]
        up_left = w_ref[0] * shift_lanes(above, 2)
        up_right = w_ref[2] * above
        down_left = w_ref[6] * below
        down_right = w_ref[8] * shift_lanes(below, width - 2)
        for k in range(3):
            if first:
                down_left = jnp.where(lane == side - 1 + k * side, 0.0, down_left)
                down_right = jnp.where(lane == 2 * side - 2 + k * side, 0.0, down_right)
            if last:
                up_left = jnp.where(lane == k * side, 0.0, up_left)
                up_right = jnp.where(lane == side - 1 + k * side, 0.0, up_right)
        total = w_ref[9] + w_ref[4] * here
        total = total + (up_right + down_left)
        total = total + (w_ref[1] * shift_lanes(above, 1) + w_ref[3] * shift_lanes(here, 1))
        total = total + (w_ref[5] * shift_lanes(here, width - 1) + w_ref[7] * shift_lanes(below, width - 1))
        total = total + (up_left + down_right)
        m_ref[q, u] = total.astype(jnp.bfloat16).astype(jnp.float32)

    for q in range(quads):
        depthwise(q, 0, first=True)

        def inner(u, carry, q=q):
            depthwise(q, u + 1)
            return carry

        fold(side - 2, inner, 0, unroll)
        depthwise(q, side - 1, last=True)

    north_cap, south_cap = lane >= 3 * side, lane < side - 1
    northern = lane >= 2 * side
    arc = jnp.where(north_cap, width - 1 - lane, jnp.where(south_cap, lane + 1, side))
    equator = jnp.logical_not(north_cap | south_cap)
    steps = []
    step = 1
    while step < side:
        steps.append(step)
        step *= 2
    has_step = {step: (arc & step) != 0 for step in steps}
    for j in range(quads):
        back = (quads - j) % quads
        for d in range(REACH):
            head_ref[j, d] = jnp.where(northern, m_ref[j, d], m_ref[back, side - 1 - d])

        def join(d, carry, j=j, back=back):
            tail_ref[j, d] = jnp.where(northern, m_ref[back, side - 1 - d], m_ref[j, d])
            return carry

        fold(side, join, 0, unroll)

    def sheared(inputs):
        seen = {}

        def line(level, t):
            if level == len(steps):
                return inputs.get(t)
            if (level, t) not in seen:
                step = steps[level]
                still, moved = line(level + 1, t), line(level + 1, t - step)
                if still is not None and moved is not None:
                    moved = jnp.where(has_step[step], moved, still)
                seen[level, t] = still if moved is None else moved
            return seen[level, t]

        return lambda t: line(0, t)

    def extend(j, carry):
        back = wrap(quads - j, quads)
        forth_strip, back_strip = wrap(j - 1, quads), wrap(quads + 1 - j, quads)
        heads, tails = {}, {}
        for d in range(REACH):
            line = head_ref[j, d]
            for a in range(1, min(d + 1, REACH)):
                line = jnp.where(arc == a, head_ref[wrap(j + d // a, quads), d % a], line)
            heads[d] = line
        for d in range(1, side):
            tails[d] = tail_ref[j, d]
        for d in range(side, side + REACH - 1):
            line = None
            for a in range(1, side + REACH - d):
                place = d - side + a
                moved = tail_ref[wrap(j + place // a, quads), side - a + place % a]
                line = moved if line is None else jnp.where(arc == a, moved, line)
            tails[d] = line
        head, tail = sheared(heads), sheared(tails)
        for t in range(DILATION, side + REACH):
            line = head(t)
            if t < side:
                ahead = jnp.where(lane >= width - 1 - t, line, m_ref[forth_strip, t])
                behind = jnp.where(lane < t, line, m_ref[back_strip, side - 1 - t])
            else:
                end = tail(t)
                ahead = jnp.where(south_cap, end, end if line is None else line)
                behind = jnp.where(north_cap, end, end if line is None else line)
                ahead = jnp.where(equator, m_ref[j, t - side], ahead)
                behind = jnp.where(equator, m_ref[back, 2 * side - 1 - t], behind)
            ahead_ref[forth_strip, t - DILATION] = ahead
            behind_ref[back_strip, t - DILATION] = behind
        return carry

    fold(quads, extend, 0, unroll)

    half = TAPS // 2

    def zonal(q, u):
        total = w_ref[17] + w_ref[10 + half] * m_ref[q, u]
        for k in range(1, half + 1):
            total = total + w_ref[10 + half + k] * ahead_ref[q, u + DILATION * (k - 1)]
            total = total + w_ref[10 + half - k] * behind_ref[q, side - 1 - u + DILATION * (k - 1)]
        return total

    def spread(sub, carry):
        seen = {}

        def row(q, local):
            q %= quads
            if (q, local) not in seen:
                seen[q, local] = zonal(q, side - 1 - sub * rows - local)
            return seen[q, local]

        for group in range(rows // 4):
            first = 4 * group
            y = sub * rows + first
            aligned = [
                [shift_lanes(row(q, first + at), wrap(width - y - at, width)) for q in range(quads)]
                for at in range(3)
            ]
            for q in range(quads):
                for at in range(3):
                    rest = row(q + 1 if at == 0 else q, first + 3)
                    rest = shift_lanes(rest, wrap((3 - at) * side - y - 3 + width, width))
                    block = jnp.where(
                        lane < side,
                        aligned[at][(q + 1) % quads],
                        jnp.where(lane < 3 * side, aligned[at][q], rest),
                    )
                    b = 3 * group + at
                    o_ref[q * subs + sub, :, b * width : (b + 1) * width] = block.astype(
                        jnp.bfloat16
                    )
        return carry

    fold(subs, spread, 0, unroll)


def lay_out(share, axes, params, columns, table, w_ref):
    first = 0
    for source in params:
        table[first : first + source.shape[0], :] = source[...]
        first += source.shape[0]
    columns[0 : table.shape[1], :] = table[...].T
    device = lax.axis_index(axes[0]) * lax.axis_size(axes[1]) + lax.axis_index(axes[1])
    start = device * share
    if share % 8 == 0:
        start = pl.multiple_of(start, 8)
    mine = columns[pl.ds(start, w_ref.shape[1]), :]
    for k in range(w_ref.shape[0]):
        w_ref[k] = jnp.broadcast_to(mine[:, k : k + 1], w_ref.shape[1:])


def pack_kernel(x_hbm, *refs):
    params, o_ref, held, x_vmem, x_sems, sems = refs[:6], refs[6], refs[7:13], refs[13], refs[14], refs[15]
    rows, _, side, channels = x_vmem.shape
    order = [at for at in range(rows) if at % 4 == 3] + [at for at in range(rows) if at % 4 != 3]
    loads = [
        pltpu.make_async_copy(x_hbm.at[:, at], x_vmem.at[at], x_sems.at[at]) for at in order
    ]
    small = [
        pltpu.make_async_copy(source, target, sems.at[i])
        for i, (source, target) in enumerate(zip(params, held, strict=True))
    ]
    for copy in small + loads:
        copy.start()
    for copy in small + loads:
        copy.wait()
    width = 4 * side
    for block in range(3 * rows // 4):
        pieces = [x_vmem[local, face] for face, local in (piece_at(block, k) for k in range(4))]
        o_ref[:, block * width : (block + 1) * width] = jnp.concatenate(pieces, 0).T


def mlp_kernel(z_ref, x_ref, gain_ref, scale_ref, w_in_ref, w_out_ref, o_hbm, o_vmem, sems):
    parts, slots, side, _ = o_vmem.shape
    width = slots * side
    gain, scale = gain_ref[...], scale_ref[...]
    stores = []
    for i in range(parts):
        values = z_ref[:, i * width : (i + 1) * width].astype(jnp.float32)
        mean = jnp.mean(values, 0, keepdims=True)
        values = values - mean
        spread = jnp.mean(jnp.square(values), 0, keepdims=True)
        values = values * lax.rsqrt(spread + EPSILON)
        normed = (values.T * gain).astype(jnp.bfloat16)
        inner = jnp.dot(normed, w_in_ref[...], preferred_element_type=jnp.float32)
        hidden = (0.5 * inner * (1.0 + lax.erf(inner * 0.5**0.5))).astype(jnp.bfloat16)
        branch = jnp.dot(hidden, w_out_ref[...], preferred_element_type=jnp.float32)
        for k in range(slots):
            face, local = piece_at(i, k)
            source = x_ref[face, local].astype(jnp.float32)
            place = face if k < slots - 1 else k
            o_vmem[i, place] = (source + scale * branch[k * side : (k + 1) * side]).astype(jnp.bfloat16)
        line = piece_at(i, 0)[1]
        face, local = piece_at(i, slots - 1)
        for at, (source, target) in enumerate(
            (
                (o_vmem.at[i, pl.ds(0, slots - 1)], o_hbm.at[:, line]),
                (o_vmem.at[i, slots - 1], o_hbm.at[face, local]),
            )
        ):
            store = pltpu.make_async_copy(source, target, sems.at[2 * i + at])
            store.start()
            stores.append(store)
    for store in stores:
        store.wait()


def shards(
    field, dw_kernel, dw_bias, zonal_kernel, zonal_bias, norm_gain, w_in, w_out, layer_scale
):
    faces, _, rows, side, channels = field.shape
    quads, subs = lax.axis_size("face"), lax.axis_size("sub")
    devices = quads * subs
    share = channels // devices
    cells = faces * rows * side
    width = quads * side
    lanes = -(-cells // width) * width
    chans = -(-share // 8) * 8
    vmem = pl.BlockSpec(memory_space=pltpu.VMEM)
    small = pltpu.CompilerParams(vmem_limit_bytes=2**20 + 24 * cells * channels)
    field_bytes = 4 * devices * chans * lanes
    large = pltpu.CompilerParams(vmem_limit_bytes=2**20 + 9 * field_bytes)

    local = field.reshape(faces, rows, side, channels)
    hbm = pl.BlockSpec(memory_space=pltpu.HBM)
    params = (
        dw_kernel, dw_bias[None], zonal_kernel, zonal_bias[None], norm_gain[None], layer_scale[None]
    )
    taps = sum(p.shape[0] for p in params[:4])
    packed, *params = pl.pallas_call(
        pack_kernel,
        out_shape=(
            jax.ShapeDtypeStruct((channels, cells), jnp.bfloat16),
            *(jax.ShapeDtypeStruct(p.shape, jnp.float32) for p in params),
        ),
        in_specs=[hbm] * 7,
        out_specs=(vmem,) * 7,
        scratch_shapes=[
            pltpu.VMEM((rows, faces, side, channels), jnp.bfloat16),
            pltpu.SemaphoreType.DMA((rows,)),
            pltpu.SemaphoreType.DMA((len(params),)),
        ],
        compiler_params=small,
        name="pack",
    )(*(pltpu.with_memory_space_constraint(array, pltpu.HBM) for array in (local, *params)))
    sent = lax.all_to_all(
        packed.reshape(devices, share, cells), ("face", "sub"), split_axis=0, concat_axis=0, tiled=True
    )
    sent = jnp.pad(sent, ((0, 0), (0, chans - share), (0, lanes - cells)))

    extra = side + REACH - DILATION
    zonal = pl.pallas_call(
        functools.partial(conv_kernel, quads, subs, side, rows, share, ("face", "sub")),
        out_shape=jax.ShapeDtypeStruct((devices, chans, lanes), jnp.bfloat16),
        in_specs=[vmem] * 5,
        out_specs=vmem,
        scratch_shapes=[
            pltpu.VMEM((quads, side + 2, chans, width), jnp.float32),
            pltpu.VMEM((quads, side, chans, width), jnp.float32),
            pltpu.VMEM((quads, extra, chans, width), jnp.float32),
            pltpu.VMEM((quads, extra, chans, width), jnp.float32),
            pltpu.VMEM((quads, REACH, chans, width), jnp.float32),
            pltpu.VMEM((quads, side, chans, width), jnp.float32),
            pltpu.VMEM((channels + chans, 128), jnp.float32),
            pltpu.VMEM((128, channels), jnp.float32),
            pltpu.VMEM((taps, chans, width), jnp.float32),
        ],
        compiler_params=large,
        name="convs",
    )(sent, *params[:4])
    zonal = zonal[:, :share, :cells]
    returned = lax.all_to_all(zonal, ("face", "sub"), split_axis=0, concat_axis=0, tiled=True)

    output = pl.pallas_call(
        mlp_kernel,
        out_shape=jax.ShapeDtypeStruct(local.shape, jnp.bfloat16),
        in_specs=[vmem] * 6,
        out_specs=hbm,
        scratch_shapes=[
            pltpu.VMEM((cells // width, quads, side, channels), jnp.bfloat16),
            pltpu.SemaphoreType.DMA((2 * cells // width,)),
        ],
        compiler_params=small,
        name="mlp",
    )(returned.reshape(channels, cells), local, *params[4:], w_in, w_out)
    return output.reshape(field.shape)


def solution(mesh):
    in_specs = (P(None, "face", "sub", None, None), P(), P(), P(), P(), P(), P(), P(), P())
    out_specs = P(None, "face", "sub", None, None)
    return jax.shard_map(shards, mesh=mesh, in_specs=in_specs, out_specs=out_specs, check_vma=False)
```

```python
import functools

import jax
import jax.numpy as jnp
from jax import lax
from jax.experimental import pallas as pl
from jax.experimental.pallas import tpu as pltpu
from jax.sharding import PartitionSpec as P

TAPS = 7
DILATION = 4
REACH = DILATION * (TAPS // 2)
EPSILON = 1e-06


def fold(count, body, carry, unroll):
    if unroll:
        for i in range(count):
            carry = body(i, carry)
        return carry
    return lax.fori_loop(0, count, body, carry)


def wrap(value, size):
    if isinstance(value, int):
        return value % size
    return lax.rem(value + size, size)


def shift_lanes(values, shift):
    width = values.shape[-1]
    if isinstance(shift, int):
        shift %= width
        if shift == 0:
            return values
    return pltpu.roll(values, shift, values.ndim - 1)


def piece_at(block, slot, faces=3):
    group, at = divmod(block, faces)
    first = group * (faces + 1)
    if slot < faces:
        return faces - 1 - slot, first + at
    return faces - 1 - at, first + faces


def conv_kernel(
    quads, subs, side, rows, share, axes, x_ref, dw_ref, dw_bias_ref, zonal_ref, zonal_bias_ref, o_ref,
    e_ref, m_ref, ahead_ref, behind_ref, columns, table, w_ref
):
    lay_out(share, axes, (dw_ref, dw_bias_ref, zonal_ref, zonal_bias_ref), columns, table, w_ref)
    width = quads * side
    chans = x_ref.shape[1]
    unroll = width <= 128
    lane = lax.broadcasted_iota(jnp.int32, (chans, width), 1)
    blocks = 3 * rows // quads

    def load(source):
        return [
            x_ref[source, :, b * width : (b + 1) * width].astype(jnp.float32)
            for b in range(blocks)
        ]

    def plain_row(held, held_before, sub, local):
        group, at = divmod(local, 4)
        y = sub * rows + local
        first = 3 * group
        if at < 3:
            row = jnp.where(lane < side, held_before[first + at], held[first + at])
            return shift_lanes(row, y)
        south = shift_lanes(held_before[first], wrap(y - 3 * side, width))
        middle = shift_lanes(held[first + 1], wrap(y - 2 * side, width))
        north = shift_lanes(held[first + 2], wrap(y - side, width))
        return jnp.where(lane < y + side, south, jnp.where(lane < y + 2 * side, middle, north))

    last_held = [load(q * subs + subs - 1) for q in range(quads)]
    first_held = [load(q * subs) for q in range(quads)]
    beyond_right, beyond_left = [], []
    for q in range(quads):
        low = plain_row(last_held[q], last_held[q - 1], subs - 1, rows - 1)
        top = plain_row(first_held[q], first_held[q - 1], 0, 0)
        beyond_right.append(shift_lanes(low, 1))
        beyond_left.append(shift_lanes(top, width - 1))

    def build(sub, diagonals):
        diagonals = list(diagonals)
        held = [load(q * subs + sub) for q in range(quads)]
        for q in range(quads):
            for local in range(rows):
                y = sub * rows + local
                row = plain_row(held[q], held[q - 1], sub, local)
                diagonals[2 * q] = jnp.where(lane < y, diagonals[2 * q], row)
                diagonals[2 * q + 1] = jnp.where(
                    lane < y + 3 * side - 1, diagonals[2 * q + 1], row
                )
                row = jnp.where(lane < y + 3 * side, row, beyond_right[(q + 1) % quads])
                row = jnp.where(lane == wrap(y - 1, width), beyond_left[q - 1], row) if not isinstance(y, int) or y == 0 else jnp.where(lane < y, beyond_left[q - 1], row)
                e_ref[q, side - y] = row
        return tuple(diagonals)

    blank = jnp.zeros((chans, width), jnp.float32)
    diagonals = fold(subs, build, (blank,) * (2 * quads), unroll)
    for q in range(quads):
        after = (q + 1) % quads
        before = (q - 1) % quads
        e_ref[q, 0] = jnp.where(
            lane < 3 * side, e_ref[before, side], shift_lanes(diagonals[2 * before + 1], 1)
        )
        e_ref[q, side + 1] = jnp.where(
            (lane >= side - 1) & (lane < 3 * side - 1),
            e_ref[after, 1],
            shift_lanes(diagonals[2 * after], width - 1),
        )

    def depthwise(q, u, first=False, last=False):
        below, here, above = e_ref[q, u], e_ref[q, u + 1], e_ref[q, u + 2]
        up_left = w_ref[0] * shift_lanes(above, 2)
        up_right = w_ref[2] * above
        down_left = w_ref[6] * below
        down_right = w_ref[8] * shift_lanes(below, width - 2)
        for k in range(3):
            if first:
                down_left = jnp.where(lane == side - 1 + k * side, 0.0, down_left)
                down_right = jnp.where(lane == 2 * side - 2 + k * side, 0.0, down_right)
            if last:
                up_left = jnp.where(lane == k * side, 0.0, up_left)
                up_right = jnp.where(lane == side - 1 + k * side, 0.0, up_right)
        total = w_ref[9] + w_ref[4] * here
        total = total + (up_right + down_left)
        total = total + (w_ref[1] * shift_lanes(above, 1) + w_ref[3] * shift_lanes(here, 1))
        total = total + (w_ref[5] * shift_lanes(here, width - 1) + w_ref[7] * shift_lanes(below, width - 1))
        total = total + (up_left + down_right)
        m_ref[q, u] = total.astype(jnp.bfloat16).astype(jnp.float32)

    for q in range(quads):
        depthwise(q, 0, first=True)

        def inner(u, carry, q=q):
            depthwise(q, u + 1)
            return carry

        fold(side - 2, inner, 0, unroll)
        depthwise(q, side - 1, last=True)

    north_cap, south_cap = lane >= 3 * side, lane < side - 1
    northern = lane >= 2 * side
    arc = jnp.where(north_cap, width - 1 - lane, jnp.where(south_cap, lane + 1, side))
    equator = jnp.logical_not(north_cap | south_cap)
    steps = []
    step = 1
    while step < side:
        steps.append(step)
        step *= 2
    has_step = {step: (arc & step) != 0 for step in steps}
    kept = {}

    def merged(j, d, tail):
        key = (j, d, tail)
        if unroll and key in kept:
            return kept[key]
        forth, back = m_ref[j, d], m_ref[wrap(quads - j, quads), side - 1 - d]
        line = jnp.where(northern, back, forth) if tail else jnp.where(northern, forth, back)
        if unroll:
            kept[key] = line
        return line

    def sheared(inputs):
        seen = {}

        def line(level, t):
            if level == len(steps):
                return inputs.get(t)
            if (level, t) not in seen:
                step = steps[level]
                still, moved = line(level + 1, t), line(level + 1, t - step)
                if still is not None and moved is not None:
                    moved = jnp.where(has_step[step], moved, still)
                seen[level, t] = still if moved is None else moved
            return seen[level, t]

        return lambda t: line(0, t)

    def extend(j, carry):
        back = wrap(quads - j, quads)
        forth_strip, back_strip = wrap(j - 1, quads), wrap(quads + 1 - j, quads)
        heads, tails = {}, {}
        for d in range(REACH):
            line = merged(j, d, False)
            for a in range(1, min(d + 1, REACH)):
                line = jnp.where(arc == a, merged(wrap(j + d // a, quads), d % a, False), line)
            heads[d] = line
        for d in range(1, side):
            tails[d] = merged(j, d, True)
        for d in range(side, side + REACH - 1):
            line = None
            for a in range(1, side + REACH - d):
                place = d - side + a
                moved = merged(wrap(j + place // a, quads), side - a + place % a, True)
                line = moved if line is None else jnp.where(arc == a, moved, line)
            tails[d] = line
        head, tail = sheared(heads), sheared(tails)
        for t in range(DILATION, side + REACH):
            line = head(t)
            if t < side:
                ahead = jnp.where(lane >= width - 1 - t, line, m_ref[forth_strip, t])
                behind = jnp.where(lane < t, line, m_ref[back_strip, side - 1 - t])
            else:
                end = tail(t)
                ahead = jnp.where(south_cap, end, end if line is None else line)
                behind = jnp.where(north_cap, end, end if line is None else line)
                ahead = jnp.where(equator, m_ref[j, t - side], ahead)
                behind = jnp.where(equator, m_ref[back, 2 * side - 1 - t], behind)
            ahead_ref[forth_strip, t - DILATION] = ahead
            behind_ref[back_strip, t - DILATION] = behind
        return carry

    fold(quads, extend, 0, unroll)

    half = TAPS // 2

    def zonal(q, u):
        total = w_ref[17] + w_ref[10 + half] * m_ref[q, u]
        for k in range(1, half + 1):
            pair = w_ref[10 + half + k] * ahead_ref[q, u + DILATION * (k - 1)]
            pair = pair + w_ref[10 + half - k] * behind_ref[q, side - 1 - u + DILATION * (k - 1)]
            total = total + pair
        return total

    def spread(sub, carry):
        seen = {}

        def row(q, local):
            q %= quads
            if (q, local) not in seen:
                seen[q, local] = zonal(q, side - 1 - sub * rows - local)
            return seen[q, local]

        for group in range(rows // 4):
            first = 4 * group
            y = sub * rows + first
            aligned = [
                [shift_lanes(row(q, first + at), wrap(width - y - at, width)) for q in range(quads)]
                for at in range(3)
            ]
            for q in range(quads):
                for at in range(3):
                    rest = row(q + 1 if at == 0 else q, first + 3)
                    rest = shift_lanes(rest, wrap((3 - at) * side - y - 3 + width, width))
                    block = jnp.where(
                        lane < side,
                        aligned[at][(q + 1) % quads],
                        jnp.where(lane < 3 * side, aligned[at][q], rest),
                    )
                    b = 3 * group + at
                    o_ref[q * subs + sub, :, b * width : (b + 1) * width] = block.astype(
                        jnp.bfloat16
                    )
        return carry

    fold(subs, spread, 0, unroll)


def lay_out(share, axes, params, columns, table, w_ref):
    first = 0
    for source in params:
        table[first : first + source.shape[0], :] = source[...]
        first += source.shape[0]
    columns[0 : table.shape[1], :] = table[...].T
    device = lax.axis_index(axes[0]) * lax.axis_size(axes[1]) + lax.axis_index(axes[1])
    start = device * share
    if share % 8 == 0:
        start = pl.multiple_of(start, 8)
    mine = columns[pl.ds(start, w_ref.shape[1]), :]
    for k in range(w_ref.shape[0]):
        w_ref[k] = jnp.broadcast_to(mine[:, k : k + 1], w_ref.shape[1:])


def pack_kernel(x_hbm, *refs):
    params, o_ref, held, x_vmem, x_sems, sems = refs[:6], refs[6], refs[7:13], refs[13], refs[14], refs[15]
    rows, _, side, channels = x_vmem.shape
    order = [at for at in range(rows) if at % 4 == 3] + [at for at in range(rows) if at % 4 != 3]
    loads = [
        pltpu.make_async_copy(x_hbm.at[:, at], x_vmem.at[at], x_sems.at[at]) for at in order
    ]
    small = [
        pltpu.make_async_copy(source, target, sems.at[i])
        for i, (source, target) in enumerate(zip(params, held, strict=True))
    ]
    for copy in small + loads:
        copy.start()
    for copy in small + loads:
        copy.wait()
    width = 4 * side
    for block in range(3 * rows // 4):
        pieces = [x_vmem[local, face] for face, local in (piece_at(block, k) for k in range(4))]
        o_ref[:, block * width : (block + 1) * width] = jnp.concatenate(pieces, 0).T


def mlp_kernel(z_ref, x_ref, gain_ref, scale_ref, w_in_ref, w_out_ref, o_hbm, o_vmem, sems):
    parts, slots, side, _ = o_vmem.shape
    width = slots * side
    gain, scale = gain_ref[...], scale_ref[...]
    stores = []
    for i in range(parts):
        values = z_ref[:, i * width : (i + 1) * width].astype(jnp.float32)
        mean = jnp.mean(values, 0, keepdims=True)
        values = values - mean
        spread = jnp.mean(jnp.square(values), 0, keepdims=True)
        values = values * lax.rsqrt(spread + EPSILON)
        normed = (values.T * gain).astype(jnp.bfloat16)
        inner = jnp.dot(normed, w_in_ref[...], preferred_element_type=jnp.float32)
        hidden = (0.5 * inner * (1.0 + lax.erf(inner * 0.5**0.5))).astype(jnp.bfloat16)
        branch = jnp.dot(hidden, w_out_ref[...], preferred_element_type=jnp.float32)
        for k in range(slots):
            face, local = piece_at(i, k)
            source = x_ref[face, local].astype(jnp.float32)
            place = face if k < slots - 1 else k
            o_vmem[i, place] = (source + scale * branch[k * side : (k + 1) * side]).astype(jnp.bfloat16)
        line = piece_at(i, 0)[1]
        face, local = piece_at(i, slots - 1)
        for at, (source, target) in enumerate(
            (
                (o_vmem.at[i, pl.ds(0, slots - 1)], o_hbm.at[:, line]),
                (o_vmem.at[i, slots - 1], o_hbm.at[face, local]),
            )
        ):
            store = pltpu.make_async_copy(source, target, sems.at[2 * i + at])
            store.start()
            stores.append(store)
    for store in stores:
        store.wait()


def shards(
    field, dw_kernel, dw_bias, zonal_kernel, zonal_bias, norm_gain, w_in, w_out, layer_scale
):
    faces, _, rows, side, channels = field.shape
    quads, subs = lax.axis_size("face"), lax.axis_size("sub")
    devices = quads * subs
    share = channels // devices
    cells = faces * rows * side
    width = quads * side
    lanes = -(-cells // width) * width
    chans = -(-share // 8) * 8
    vmem = pl.BlockSpec(memory_space=pltpu.VMEM)
    small = pltpu.CompilerParams(vmem_limit_bytes=2**20 + 24 * cells * channels)
    field_bytes = 4 * devices * chans * lanes
    large = pltpu.CompilerParams(vmem_limit_bytes=2**20 + 9 * field_bytes)

    local = field.reshape(faces, rows, side, channels)
    hbm = pl.BlockSpec(memory_space=pltpu.HBM)
    params = (
        dw_kernel, dw_bias[None], zonal_kernel, zonal_bias[None], norm_gain[None], layer_scale[None]
    )
    taps = sum(p.shape[0] for p in params[:4])
    packed, *params = pl.pallas_call(
        pack_kernel,
        out_shape=(
            jax.ShapeDtypeStruct((channels, cells), jnp.bfloat16),
            *(jax.ShapeDtypeStruct(p.shape, jnp.float32) for p in params),
        ),
        in_specs=[hbm] * 7,
        out_specs=(vmem,) * 7,
        scratch_shapes=[
            pltpu.VMEM((rows, faces, side, channels), jnp.bfloat16),
            pltpu.SemaphoreType.DMA((rows,)),
            pltpu.SemaphoreType.DMA((len(params),)),
        ],
        compiler_params=small,
        name="pack",
    )(*(pltpu.with_memory_space_constraint(array, pltpu.HBM) for array in (local, *params)))
    sent = lax.all_to_all(
        packed.reshape(devices, share, cells), ("face", "sub"), split_axis=0, concat_axis=0, tiled=True
    )
    sent = jnp.pad(sent, ((0, 0), (0, chans - share), (0, lanes - cells)))

    extra = side + REACH - DILATION
    zonal = pl.pallas_call(
        functools.partial(conv_kernel, quads, subs, side, rows, share, ("face", "sub")),
        out_shape=jax.ShapeDtypeStruct((devices, chans, lanes), jnp.bfloat16),
        in_specs=[vmem] * 5,
        out_specs=vmem,
        scratch_shapes=[
            pltpu.VMEM((quads, side + 2, chans, width), jnp.float32),
            pltpu.VMEM((quads, side, chans, width), jnp.float32),
            pltpu.VMEM((quads, extra, chans, width), jnp.float32),
            pltpu.VMEM((quads, extra, chans, width), jnp.float32),
            pltpu.VMEM((channels + chans, 128), jnp.float32),
            pltpu.VMEM((128, channels), jnp.float32),
            pltpu.VMEM((taps, chans, width), jnp.float32),
        ],
        compiler_params=large,
        name="convs",
    )(sent, *params[:4])
    zonal = zonal[:, :share, :cells]
    returned = lax.all_to_all(zonal, ("face", "sub"), split_axis=0, concat_axis=0, tiled=True)

    output = pl.pallas_call(
        mlp_kernel,
        out_shape=jax.ShapeDtypeStruct(local.shape, jnp.bfloat16),
        in_specs=[vmem] * 6,
        out_specs=hbm,
        scratch_shapes=[
            pltpu.VMEM((cells // width, quads, side, channels), jnp.bfloat16),
            pltpu.SemaphoreType.DMA((2 * cells // width,)),
        ],
        compiler_params=small,
        name="mlp",
    )(returned.reshape(channels, cells), local, *params[4:], w_in, w_out)
    return output.reshape(field.shape)


def solution(mesh):
    in_specs = (P(None, "face", "sub", None, None), P(), P(), P(), P(), P(), P(), P(), P())
    out_specs = P(None, "face", "sub", None, None)
    return jax.shard_map(shards, mesh=mesh, in_specs=in_specs, out_specs=out_specs, check_vma=False)
```

```python
import functools

import jax
import jax.numpy as jnp
from jax import lax
from jax.experimental import pallas as pl
from jax.experimental.pallas import tpu as pltpu
from jax.sharding import PartitionSpec as P

TAPS = 7
DILATION = 4
REACH = DILATION * (TAPS // 2)
EPSILON = 1e-06


def fold(count, body, carry, unroll):
    if unroll:
        for i in range(count):
            carry = body(i, carry)
        return carry
    return lax.fori_loop(0, count, body, carry)


def wrap(value, size):
    if isinstance(value, int):
        return value % size
    return lax.rem(value + size, size)


def shift_lanes(values, shift):
    width = values.shape[-1]
    if isinstance(shift, int):
        shift %= width
        if shift == 0:
            return values
    return pltpu.roll(values, shift, values.ndim - 1)


def piece_at(block, slot, faces=3):
    group, at = divmod(block, faces)
    first = group * (faces + 1)
    if slot < faces:
        return faces - 1 - slot, first + at
    return faces - 1 - at, first + faces


def conv_kernel(
    quads, subs, side, rows, share, axes, x_ref, dw_ref, dw_bias_ref, zonal_ref, zonal_bias_ref, o_ref,
    e_ref, m_ref, ahead_ref, behind_ref, columns, table, w_ref
):
    width = quads * side
    chans = x_ref.shape[1]
    unroll = width <= 128
    lane = lax.broadcasted_iota(jnp.int32, (chans, width), 1)
    blocks = 3 * rows // quads

    def load(source):
        return [
            x_ref[source, :, b * width : (b + 1) * width].astype(jnp.float32)
            for b in range(blocks)
        ]

    def plain_row(held, held_before, sub, local):
        group, at = divmod(local, 4)
        y = sub * rows + local
        first = 3 * group
        if at < 3:
            row = jnp.where(lane < side, held_before[first + at], held[first + at])
            return shift_lanes(row, y)
        south = shift_lanes(held_before[first], wrap(y - 3 * side, width))
        middle = shift_lanes(held[first + 1], wrap(y - 2 * side, width))
        north = shift_lanes(held[first + 2], wrap(y - side, width))
        return jnp.where(lane < y + side, south, jnp.where(lane < y + 2 * side, middle, north))

    last_held = [load(q * subs + subs - 1) for q in range(quads)]
    first_held = [load(q * subs) for q in range(quads)]
    beyond_right, beyond_left = [], []
    for q in range(quads):
        low = plain_row(last_held[q], last_held[q - 1], subs - 1, rows - 1)
        top = plain_row(first_held[q], first_held[q - 1], 0, 0)
        beyond_right.append(shift_lanes(low, 1))
        beyond_left.append(shift_lanes(top, width - 1))

    def build(sub, diagonals):
        diagonals = list(diagonals)
        held = [load(q * subs + sub) for q in range(quads)]
        for q in range(quads):
            for local in range(rows):
                y = sub * rows + local
                row = plain_row(held[q], held[q - 1], sub, local)
                diagonals[2 * q] = jnp.where(lane < y, diagonals[2 * q], row)
                diagonals[2 * q + 1] = jnp.where(
                    lane < y + 3 * side - 1, diagonals[2 * q + 1], row
                )
                row = jnp.where(lane < y + 3 * side, row, beyond_right[(q + 1) % quads])
                row = jnp.where(lane == wrap(y - 1, width), beyond_left[q - 1], row) if not isinstance(y, int) or y == 0 else jnp.where(lane < y, beyond_left[q - 1], row)
                e_ref[q, side - y] = row
        return tuple(diagonals)

    blank = jnp.zeros((chans, width), jnp.float32)
    diagonals = fold(subs, build, (blank,) * (2 * quads), unroll)
    for q in range(quads):
        after = (q + 1) % quads
        before = (q - 1) % quads
        e_ref[q, 0] = jnp.where(
            lane < 3 * side, e_ref[before, side], shift_lanes(diagonals[2 * before + 1], 1)
        )
        e_ref[q, side + 1] = jnp.where(
            (lane >= side - 1) & (lane < 3 * side - 1),
            e_ref[after, 1],
            shift_lanes(diagonals[2 * after], width - 1),
        )

    lay_out(share, axes, (dw_ref, dw_bias_ref, zonal_ref, zonal_bias_ref), columns, table, w_ref)

    def depthwise(q, u, first=False, last=False):
        below, here, above = e_ref[q, u], e_ref[q, u + 1], e_ref[q, u + 2]
        up_left = w_ref[0] * shift_lanes(above, 2)
        up_right = w_ref[2] * above
        down_left = w_ref[6] * below
        down_right = w_ref[8] * shift_lanes(below, width - 2)
        for k in range(3):
            if first:
                down_left = jnp.where(lane == side - 1 + k * side, 0.0, down_left)
                down_right = jnp.where(lane == 2 * side - 2 + k * side, 0.0, down_right)
            if last:
                up_left = jnp.where(lane == k * side, 0.0, up_left)
                up_right = jnp.where(lane == side - 1 + k * side, 0.0, up_right)
        total = w_ref[9] + w_ref[4] * here
        total = total + (up_right + down_left)
        total = total + (w_ref[1] * shift_lanes(above, 1) + w_ref[3] * shift_lanes(here, 1))
        total = total + (w_ref[5] * shift_lanes(here, width - 1) + w_ref[7] * shift_lanes(below, width - 1))
        total = total + (up_left + down_right)
        m_ref[q, u] = total.astype(jnp.bfloat16).astype(jnp.float32)

    for q in range(quads):
        depthwise(q, 0, first=True)

        def inner(u, carry, q=q):
            depthwise(q, u + 1)
            return carry

        fold(side - 2, inner, 0, unroll)
        depthwise(q, side - 1, last=True)

    north_cap, south_cap = lane >= 3 * side, lane < side - 1
    northern = lane >= 2 * side
    arc = jnp.where(north_cap, width - 1 - lane, jnp.where(south_cap, lane + 1, side))
    equator = jnp.logical_not(north_cap | south_cap)
    steps = []
    step = 1
    while step < side:
        steps.append(step)
        step *= 2
    has_step = {step: (arc & step) != 0 for step in steps}
    kept = {}

    def merged(j, d, tail):
        key = (j, d, tail)
        if unroll and key in kept:
            return kept[key]
        forth, back = m_ref[j, d], m_ref[wrap(quads - j, quads), side - 1 - d]
        line = jnp.where(northern, back, forth) if tail else jnp.where(northern, forth, back)
        if unroll:
            kept[key] = line
        return line

    def sheared(inputs):
        seen = {}

        def line(level, t):
            if level == len(steps):
                return inputs.get(t)
            if (level, t) not in seen:
                step = steps[level]
                still, moved = line(level + 1, t), line(level + 1, t - step)
                if still is not None and moved is not None:
                    moved = jnp.where(has_step[step], moved, still)
                seen[level, t] = still if moved is None else moved
            return seen[level, t]

        return lambda t: line(0, t)

    def extend(j, carry):
        back = wrap(quads - j, quads)
        forth_strip, back_strip = wrap(j - 1, quads), wrap(quads + 1 - j, quads)
        heads, tails = {}, {}
        for d in range(REACH):
            line = merged(j, d, False)
            for a in range(1, min(d + 1, REACH)):
                line = jnp.where(arc == a, merged(wrap(j + d // a, quads), d % a, False), line)
            heads[d] = line
        for d in range(1, side):
            tails[d] = merged(j, d, True)
        for d in range(side, side + REACH - 1):
            line = None
            for a in range(1, side + REACH - d):
                place = d - side + a
                moved = merged(wrap(j + place // a, quads), side - a + place % a, True)
                line = moved if line is None else jnp.where(arc == a, moved, line)
            tails[d] = line
        head, tail = sheared(heads), sheared(tails)
        for t in range(DILATION, side + REACH):
            line = head(t)
            if t < side:
                ahead = jnp.where(lane >= width - 1 - t, line, m_ref[forth_strip, t])
                behind = jnp.where(lane < t, line, m_ref[back_strip, side - 1 - t])
            else:
                end = tail(t)
                ahead = jnp.where(south_cap, end, end if line is None else line)
                behind = jnp.where(north_cap, end, end if line is None else line)
                ahead = jnp.where(equator, m_ref[j, t - side], ahead)
                behind = jnp.where(equator, m_ref[back, 2 * side - 1 - t], behind)
            ahead_ref[forth_strip, t - DILATION] = ahead
            behind_ref[back_strip, t - DILATION] = behind
        return carry

    fold(quads, extend, 0, unroll)

    half = TAPS // 2

    def zonal(q, u):
        total = w_ref[17] + w_ref[10 + half] * m_ref[q, u]
        for k in range(1, half + 1):
            pair = w_ref[10 + half + k] * ahead_ref[q, u + DILATION * (k - 1)]
            pair = pair + w_ref[10 + half - k] * behind_ref[q, side - 1 - u + DILATION * (k - 1)]
            total = total + pair
        return total

    def spread(sub, carry):
        seen = {}

        def row(q, local):
            q %= quads
            if (q, local) not in seen:
                seen[q, local] = zonal(q, side - 1 - sub * rows - local)
            return seen[q, local]

        for group in range(rows // 4):
            first = 4 * group
            y = sub * rows + first
            aligned = [
                [shift_lanes(row(q, first + at), wrap(width - y - at, width)) for q in range(quads)]
                for at in range(3)
            ]
            for q in range(quads):
                for at in range(3):
                    rest = row(q + 1 if at == 0 else q, first + 3)
                    rest = shift_lanes(rest, wrap((3 - at) * side - y - 3 + width, width))
                    block = jnp.where(
                        lane < side,
                        aligned[at][(q + 1) % quads],
                        jnp.where(lane < 3 * side, aligned[at][q], rest),
                    )
                    b = 3 * group + at
                    o_ref[q * subs + sub, :, b * width : (b + 1) * width] = block.astype(
                        jnp.bfloat16
                    )
        return carry

    fold(subs, spread, 0, unroll)


def lay_out(share, axes, params, columns, table, w_ref):
    first = 0
    for source in params:
        table[first : first + source.shape[0], :] = source[...]
        first += source.shape[0]
    columns[0 : table.shape[1], :] = table[...].T
    device = lax.axis_index(axes[0]) * lax.axis_size(axes[1]) + lax.axis_index(axes[1])
    start = device * share
    if share % 8 == 0:
        start = pl.multiple_of(start, 8)
    mine = columns[pl.ds(start, w_ref.shape[1]), :]
    for k in range(w_ref.shape[0]):
        w_ref[k] = jnp.broadcast_to(mine[:, k : k + 1], w_ref.shape[1:])


def pack_kernel(x_hbm, *refs):
    params, o_ref, held, x_vmem, x_sems, sems = refs[:6], refs[6], refs[7:13], refs[13], refs[14], refs[15]
    rows, _, side, channels = x_vmem.shape
    order = [at for at in range(rows) if at % 4 == 3] + [at for at in range(rows) if at % 4 != 3]
    loads = [
        pltpu.make_async_copy(x_hbm.at[:, at], x_vmem.at[at], x_sems.at[at]) for at in order
    ]
    small = [
        pltpu.make_async_copy(source, target, sems.at[i])
        for i, (source, target) in enumerate(zip(params, held, strict=True))
    ]
    for copy in small + loads:
        copy.start()
    for copy in small + loads:
        copy.wait()
    width = 4 * side
    for block in range(3 * rows // 4):
        pieces = [x_vmem[local, face] for face, local in (piece_at(block, k) for k in range(4))]
        o_ref[:, block * width : (block + 1) * width] = jnp.concatenate(pieces, 0).T


def mlp_kernel(z_ref, x_ref, gain_ref, scale_ref, w_in_ref, w_out_ref, o_hbm, o_vmem, sems):
    parts, slots, side, _ = o_vmem.shape
    width = slots * side
    gain, scale = gain_ref[...], scale_ref[...]
    stores = []
    for i in range(parts):
        values = z_ref[:, i * width : (i + 1) * width].astype(jnp.float32)
        mean = jnp.mean(values, 0, keepdims=True)
        values = values - mean
        spread = jnp.mean(jnp.square(values), 0, keepdims=True)
        values = values * lax.rsqrt(spread + EPSILON)
        normed = (values.T * gain).astype(jnp.bfloat16)
        inner = jnp.dot(normed, w_in_ref[...], preferred_element_type=jnp.float32)
        hidden = (0.5 * inner * (1.0 + lax.erf(inner * 0.5**0.5))).astype(jnp.bfloat16)
        branch = jnp.dot(hidden, w_out_ref[...], preferred_element_type=jnp.float32)
        for k in range(slots):
            face, local = piece_at(i, k)
            source = x_ref[face, local].astype(jnp.float32)
            place = face if k < slots - 1 else k
            o_vmem[i, place] = (source + scale * branch[k * side : (k + 1) * side]).astype(jnp.bfloat16)
        line = piece_at(i, 0)[1]
        face, local = piece_at(i, slots - 1)
        for at, (source, target) in enumerate(
            (
                (o_vmem.at[i, pl.ds(0, slots - 1)], o_hbm.at[:, line]),
                (o_vmem.at[i, slots - 1], o_hbm.at[face, local]),
            )
        ):
            store = pltpu.make_async_copy(source, target, sems.at[2 * i + at])
            store.start()
            stores.append(store)
    for store in stores:
        store.wait()


def shards(
    field, dw_kernel, dw_bias, zonal_kernel, zonal_bias, norm_gain, w_in, w_out, layer_scale
):
    faces, _, rows, side, channels = field.shape
    quads, subs = lax.axis_size("face"), lax.axis_size("sub")
    devices = quads * subs
    share = channels // devices
    cells = faces * rows * side
    width = quads * side
    lanes = -(-cells // width) * width
    chans = -(-share // 8) * 8
    vmem = pl.BlockSpec(memory_space=pltpu.VMEM)
    small = pltpu.CompilerParams(vmem_limit_bytes=2**20 + 24 * cells * channels)
    field_bytes = 4 * devices * chans * lanes
    large = pltpu.CompilerParams(vmem_limit_bytes=2**20 + 9 * field_bytes)

    local = field.reshape(faces, rows, side, channels)
    hbm = pl.BlockSpec(memory_space=pltpu.HBM)
    params = (
        dw_kernel, dw_bias[None], zonal_kernel, zonal_bias[None], norm_gain[None], layer_scale[None]
    )
    taps = sum(p.shape[0] for p in params[:4])
    packed, *params = pl.pallas_call(
        pack_kernel,
        out_shape=(
            jax.ShapeDtypeStruct((channels, cells), jnp.bfloat16),
            *(jax.ShapeDtypeStruct(p.shape, jnp.float32) for p in params),
        ),
        in_specs=[hbm] * 7,
        out_specs=(vmem,) * 7,
        scratch_shapes=[
            pltpu.VMEM((rows, faces, side, channels), jnp.bfloat16),
            pltpu.SemaphoreType.DMA((rows,)),
            pltpu.SemaphoreType.DMA((len(params),)),
        ],
        compiler_params=small,
        name="pack",
    )(*(pltpu.with_memory_space_constraint(array, pltpu.HBM) for array in (local, *params)))
    sent = lax.all_to_all(
        packed.reshape(devices, share, cells), ("face", "sub"), split_axis=0, concat_axis=0, tiled=True
    )
    sent = jnp.pad(sent, ((0, 0), (0, chans - share), (0, lanes - cells)))

    extra = side + REACH - DILATION
    zonal = pl.pallas_call(
        functools.partial(conv_kernel, quads, subs, side, rows, share, ("face", "sub")),
        out_shape=jax.ShapeDtypeStruct((devices, chans, lanes), jnp.bfloat16),
        in_specs=[vmem] * 5,
        out_specs=vmem,
        scratch_shapes=[
            pltpu.VMEM((quads, side + 2, chans, width), jnp.float32),
            pltpu.VMEM((quads, side, chans, width), jnp.float32),
            pltpu.VMEM((quads, extra, chans, width), jnp.float32),
            pltpu.VMEM((quads, extra, chans, width), jnp.float32),
            pltpu.VMEM((channels + chans, 128), jnp.float32),
            pltpu.VMEM((128, channels), jnp.float32),
            pltpu.VMEM((taps, chans, width), jnp.float32),
        ],
        compiler_params=large,
        name="convs",
    )(sent, *params[:4])
    zonal = zonal[:, :share, :cells]
    returned = lax.all_to_all(zonal, ("face", "sub"), split_axis=0, concat_axis=0, tiled=True)

    output = pl.pallas_call(
        mlp_kernel,
        out_shape=jax.ShapeDtypeStruct(local.shape, jnp.bfloat16),
        in_specs=[vmem] * 6,
        out_specs=hbm,
        scratch_shapes=[
            pltpu.VMEM((cells // width, quads, side, channels), jnp.bfloat16),
            pltpu.SemaphoreType.DMA((2 * cells // width,)),
        ],
        compiler_params=small,
        name="mlp",
    )(returned.reshape(channels, cells), local, *params[4:], w_in, w_out)
    return output.reshape(field.shape)


def solution(mesh):
    in_specs = (P(None, "face", "sub", None, None), P(), P(), P(), P(), P(), P(), P(), P())
    out_specs = P(None, "face", "sub", None, None)
    return jax.shard_map(shards, mesh=mesh, in_specs=in_specs, out_specs=out_specs, check_vma=False)
```

```python
import functools

import jax
import jax.numpy as jnp
from jax import lax
from jax.experimental import pallas as pl
from jax.experimental.pallas import tpu as pltpu
from jax.sharding import PartitionSpec as P

TAPS = 7
DILATION = 4
REACH = DILATION * (TAPS // 2)
EPSILON = 1e-06


def fold(count, body, carry, unroll):
    if unroll:
        for i in range(count):
            carry = body(i, carry)
        return carry
    return lax.fori_loop(0, count, body, carry)


def wrap(value, size):
    if isinstance(value, int):
        return value % size
    return lax.rem(value + size, size)


def shift_lanes(values, shift):
    width = values.shape[-1]
    if isinstance(shift, int):
        shift %= width
        if shift == 0:
            return values
    return pltpu.roll(values, shift, values.ndim - 1)


def piece_at(block, slot, faces=3):
    group, at = divmod(block, faces)
    first = group * (faces + 1)
    if slot < faces:
        return faces - 1 - slot, first + at
    return faces - 1 - at, first + faces


def conv_kernel(
    quads, subs, side, rows, share, axes, x_ref, dw_ref, dw_bias_ref, zonal_ref, zonal_bias_ref, o_ref,
    e_ref, m_ref, ahead_ref, behind_ref, columns, table, w_ref
):
    width = quads * side
    chans = x_ref.shape[1]
    unroll = width <= 128
    lane = lax.broadcasted_iota(jnp.int32, (chans, width), 1)
    blocks = 3 * rows // quads

    def load(source):
        return [
            x_ref[source, :, b * width : (b + 1) * width].astype(jnp.float32)
            for b in range(blocks)
        ]

    def plain_row(held, held_before, sub, local):
        group, at = divmod(local, 4)
        y = sub * rows + local
        first = 3 * group
        if at < 3:
            row = jnp.where(lane < side, held_before[first + at], held[first + at])
            return shift_lanes(row, y)
        south = shift_lanes(held_before[first], wrap(y - 3 * side, width))
        middle = shift_lanes(held[first + 1], wrap(y - 2 * side, width))
        north = shift_lanes(held[first + 2], wrap(y - side, width))
        return jnp.where(lane < y + side, south, jnp.where(lane < y + 2 * side, middle, north))

    last_held = [load(q * subs + subs - 1) for q in range(quads)]
    first_held = [load(q * subs) for q in range(quads)]
    beyond_right, beyond_left = [], []
    for q in range(quads):
        low = plain_row(last_held[q], last_held[q - 1], subs - 1, rows - 1)
        top = plain_row(first_held[q], first_held[q - 1], 0, 0)
        beyond_right.append(shift_lanes(low, 1))
        beyond_left.append(shift_lanes(top, width - 1))

    def build(sub, diagonals):
        diagonals = list(diagonals)
        held = [load(q * subs + sub) for q in range(quads)]
        for q in range(quads):
            for local in range(rows):
                y = sub * rows + local
                row = plain_row(held[q], held[q - 1], sub, local)
                diagonals[2 * q] = jnp.where(lane < y, diagonals[2 * q], row)
                diagonals[2 * q + 1] = jnp.where(
                    lane < y + 3 * side - 1, diagonals[2 * q + 1], row
                )
                row = jnp.where(lane < y + 3 * side, row, beyond_right[(q + 1) % quads])
                row = jnp.where(lane == wrap(y - 1, width), beyond_left[q - 1], row) if not isinstance(y, int) or y == 0 else jnp.where(lane < y, beyond_left[q - 1], row)
                e_ref[q, side - y] = row
        return tuple(diagonals)

    blank = jnp.zeros((chans, width), jnp.float32)
    diagonals = fold(subs, build, (blank,) * (2 * quads), unroll)
    for q in range(quads):
        after = (q + 1) % quads
        before = (q - 1) % quads
        e_ref[q, 0] = jnp.where(
            lane < 3 * side, e_ref[before, side], shift_lanes(diagonals[2 * before + 1], 1)
        )
        e_ref[q, side + 1] = jnp.where(
            (lane >= side - 1) & (lane < 3 * side - 1),
            e_ref[after, 1],
            shift_lanes(diagonals[2 * after], width - 1),
        )

    lay_out(share, axes, (dw_ref, dw_bias_ref, zonal_ref, zonal_bias_ref), columns, table, w_ref)

    def depthwise(q, u, first=False, last=False):
        below, here, above = e_ref[q, u], e_ref[q, u + 1], e_ref[q, u + 2]
        up_left = w_ref[0] * shift_lanes(above, 2)
        up_right = w_ref[2] * above
        down_left = w_ref[6] * below
        down_right = w_ref[8] * shift_lanes(below, width - 2)
        for k in range(3):
            if first:
                down_left = jnp.where(lane == side - 1 + k * side, 0.0, down_left)
                down_right = jnp.where(lane == 2 * side - 2 + k * side, 0.0, down_right)
            if last:
                up_left = jnp.where(lane == k * side, 0.0, up_left)
                up_right = jnp.where(lane == side - 1 + k * side, 0.0, up_right)
        total = w_ref[9] + w_ref[4] * here
        total = total + (up_right + down_left)
        total = total + (w_ref[1] * shift_lanes(above, 1) + w_ref[3] * shift_lanes(here, 1))
        total = total + (w_ref[5] * shift_lanes(here, width - 1) + w_ref[7] * shift_lanes(below, width - 1))
        total = total + (up_left + down_right)
        m_ref[q, u] = total.astype(jnp.bfloat16).astype(jnp.float32)

    for q in range(quads):
        depthwise(q, 0, first=True)

        def inner(u, carry, q=q):
            depthwise(q, u + 1)
            return carry

        fold(side - 2, inner, 0, unroll)
        depthwise(q, side - 1, last=True)

    north_cap, south_cap = lane >= 3 * side, lane < side - 1
    northern = lane >= 2 * side
    arc = jnp.where(north_cap, width - 1 - lane, jnp.where(south_cap, lane + 1, side))
    equator = jnp.logical_not(north_cap | south_cap)
    steps = []
    step = 1
    while step < side:
        steps.append(step)
        step *= 2
    has_step = {step: (arc & step) != 0 for step in steps}
    kept = {}

    def merged(j, d, tail):
        key = (j, d, tail)
        if unroll and key in kept:
            return kept[key]
        forth, back = m_ref[j, d], m_ref[wrap(quads - j, quads), side - 1 - d]
        line = jnp.where(northern, back, forth) if tail else jnp.where(northern, forth, back)
        if unroll:
            kept[key] = line
        return line

    def sheared(inputs):
        seen = {}

        def line(level, t):
            if level == len(steps):
                return inputs.get(t)
            if (level, t) not in seen:
                step = steps[level]
                still, moved = line(level + 1, t), line(level + 1, t - step)
                if still is not None and moved is not None:
                    moved = jnp.where(has_step[step], moved, still)
                seen[level, t] = still if moved is None else moved
            return seen[level, t]

        return lambda t: line(0, t)

    def extend(j, carry):
        back = wrap(quads - j, quads)
        forth_strip, back_strip = wrap(j - 1, quads), wrap(quads + 1 - j, quads)
        heads, tails = {}, {}
        for d in range(REACH):
            line = merged(j, d, False)
            for a in range(1, min(d + 1, REACH)):
                line = jnp.where(arc == a, merged(wrap(j + d // a, quads), d % a, False), line)
            heads[d] = line
        for d in range(1, side):
            tails[d] = merged(j, d, True)
        for d in range(side, side + REACH - 1):
            line = None
            for a in range(1, side + REACH - d):
                place = d - side + a
                moved = merged(wrap(j + place // a, quads), side - a + place % a, True)
                line = moved if line is None else jnp.where(arc == a, moved, line)
            tails[d] = line
        head, tail = sheared(heads), sheared(tails)
        for t in range(DILATION, side + REACH):
            line = head(t)
            if t < side:
                ahead = jnp.where(lane >= width - 1 - t, line, m_ref[forth_strip, t])
                behind = jnp.where(lane < t, line, m_ref[back_strip, side - 1 - t])
            else:
                end = tail(t)
                ahead = jnp.where(south_cap, end, end if line is None else line)
                behind = jnp.where(north_cap, end, end if line is None else line)
                ahead = jnp.where(equator, m_ref[j, t - side], ahead)
                behind = jnp.where(equator, m_ref[back, 2 * side - 1 - t], behind)
            ahead_ref[forth_strip, t - DILATION] = ahead
            behind_ref[back_strip, t - DILATION] = behind
        return carry

    fold(quads, extend, 0, unroll)

    half = TAPS // 2

    def zonal(q, u):
        total = w_ref[17] + w_ref[10 + half] * m_ref[q, u]
        for k in range(1, half + 1):
            pair = w_ref[10 + half + k] * ahead_ref[q, u + DILATION * (k - 1)]
            pair = pair + w_ref[10 + half - k] * behind_ref[q, side - 1 - u + DILATION * (k - 1)]
            total = total + pair
        return total

    def spread(sub, carry):
        seen = {}

        def row(q, local):
            q %= quads
            if (q, local) not in seen:
                seen[q, local] = zonal(q, side - 1 - sub * rows - local)
            return seen[q, local]

        for group in range(rows // 4):
            first = 4 * group
            y = sub * rows + first
            aligned = [
                [shift_lanes(row(q, first + at), wrap(width - y - at, width)) for q in range(quads)]
                for at in range(3)
            ]
            for q in range(quads):
                for at in range(3):
                    rest = row(q + 1 if at == 0 else q, first + 3)
                    rest = shift_lanes(rest, wrap((3 - at) * side - y - 3 + width, width))
                    block = jnp.where(
                        lane < side,
                        aligned[at][(q + 1) % quads],
                        jnp.where(lane < 3 * side, aligned[at][q], rest),
                    )
                    b = 3 * group + at
                    o_ref[q * subs + sub, :, b * width : (b + 1) * width] = block.astype(
                        jnp.bfloat16
                    )
        return carry

    fold(subs, spread, 0, unroll)


def lay_out(share, axes, params, columns, table, w_ref):
    first = 0
    for source in params:
        table[first : first + source.shape[0], :] = source[...]
        first += source.shape[0]
    columns[0 : table.shape[1], :] = table[...].T
    device = lax.axis_index(axes[0]) * lax.axis_size(axes[1]) + lax.axis_index(axes[1])
    start = device * share
    if share % 8 == 0:
        start = pl.multiple_of(start, 8)
    mine = columns[pl.ds(start, w_ref.shape[1]), :]
    for k in range(w_ref.shape[0]):
        w_ref[k] = jnp.broadcast_to(mine[:, k : k + 1], w_ref.shape[1:])


def pack_kernel(x_hbm, *refs):
    params, o_ref, held, x_vmem, x_sems, sems = refs[:6], refs[6], refs[7:13], refs[13], refs[14], refs[15]
    rows, _, side, channels = x_vmem.shape
    order = [at for at in range(rows) if at % 4 == 3] + [at for at in range(rows) if at % 4 != 3]
    loads = [
        pltpu.make_async_copy(x_hbm.at[:, at], x_vmem.at[at], x_sems.at[at]) for at in order
    ]
    small = [
        pltpu.make_async_copy(source, target, sems.at[i])
        for i, (source, target) in enumerate(zip(params, held, strict=True))
    ]
    for copy in small + loads:
        copy.start()
    for copy in small + loads:
        copy.wait()
    width = 4 * side
    for block in range(3 * rows // 4):
        pieces = [x_vmem[local, face] for face, local in (piece_at(block, k) for k in range(4))]
        o_ref[:, block * width : (block + 1) * width] = jnp.concatenate(pieces, 0).T


def mlp_kernel(z_ref, x_ref, gain_ref, scale_ref, w_in_ref, w_out_ref, o_hbm, o_vmem, sems):
    _, faces, side, _ = o_vmem.shape
    slots = faces + 1
    width = slots * side
    parts = z_ref.shape[1] // width
    gain, scale = gain_ref[...], scale_ref[...]
    stores = []
    for i in range(parts):
        values = z_ref[:, i * width : (i + 1) * width].astype(jnp.float32)
        mean = jnp.mean(values, 0, keepdims=True)
        values = values - mean
        spread = jnp.mean(jnp.square(values), 0, keepdims=True)
        values = values * lax.rsqrt(spread + EPSILON)
        normed = (values.T * gain).astype(jnp.bfloat16)
        inner = jnp.dot(normed, w_in_ref[...], preferred_element_type=jnp.float32)
        hidden = (0.5 * inner * (1.0 + lax.erf(inner * 0.5**0.5))).astype(jnp.bfloat16)
        branch = jnp.dot(hidden, w_out_ref[...], preferred_element_type=jnp.float32)
        for k in range(slots):
            face, local = piece_at(i, k)
            source = x_ref[face, local].astype(jnp.float32)
            part = source + scale * branch[k * side : (k + 1) * side]
            o_vmem[local, face] = part.astype(jnp.bfloat16)
        lines = [piece_at(i, 0)[1]]
        if i % 3 == 2:
            lines.append(piece_at(i, slots - 1)[1])
        for line in lines:
            store = pltpu.make_async_copy(o_vmem.at[line], o_hbm.at[:, line], sems.at[line])
            store.start()
            stores.append(store)
    for store in stores:
        store.wait()


def shards(
    field, dw_kernel, dw_bias, zonal_kernel, zonal_bias, norm_gain, w_in, w_out, layer_scale
):
    faces, _, rows, side, channels = field.shape
    quads, subs = lax.axis_size("face"), lax.axis_size("sub")
    devices = quads * subs
    share = channels // devices
    cells = faces * rows * side
    width = quads * side
    lanes = -(-cells // width) * width
    chans = -(-share // 8) * 8
    vmem = pl.BlockSpec(memory_space=pltpu.VMEM)
    small = pltpu.CompilerParams(vmem_limit_bytes=2**20 + 24 * cells * channels)
    field_bytes = 4 * devices * chans * lanes
    large = pltpu.CompilerParams(vmem_limit_bytes=2**20 + 9 * field_bytes)

    local = field.reshape(faces, rows, side, channels)
    hbm = pl.BlockSpec(memory_space=pltpu.HBM)
    params = (
        dw_kernel, dw_bias[None], zonal_kernel, zonal_bias[None], norm_gain[None], layer_scale[None]
    )
    taps = sum(p.shape[0] for p in params[:4])
    packed, *params = pl.pallas_call(
        pack_kernel,
        out_shape=(
            jax.ShapeDtypeStruct((channels, cells), jnp.bfloat16),
            *(jax.ShapeDtypeStruct(p.shape, jnp.float32) for p in params),
        ),
        in_specs=[hbm] * 7,
        out_specs=(vmem,) * 7,
        scratch_shapes=[
            pltpu.VMEM((rows, faces, side, channels), jnp.bfloat16),
            pltpu.SemaphoreType.DMA((rows,)),
            pltpu.SemaphoreType.DMA((len(params),)),
        ],
        compiler_params=small,
        name="pack",
    )(*(pltpu.with_memory_space_constraint(array, pltpu.HBM) for array in (local, *params)))
    sent = lax.all_to_all(
        packed.reshape(devices, share, cells), ("face", "sub"), split_axis=0, concat_axis=0, tiled=True
    )
    sent = jnp.pad(sent, ((0, 0), (0, chans - share), (0, lanes - cells)))

    extra = side + REACH - DILATION
    zonal = pl.pallas_call(
        functools.partial(conv_kernel, quads, subs, side, rows, share, ("face", "sub")),
        out_shape=jax.ShapeDtypeStruct((devices, chans, lanes), jnp.bfloat16),
        in_specs=[vmem] * 5,
        out_specs=vmem,
        scratch_shapes=[
            pltpu.VMEM((quads, side + 2, chans, width), jnp.float32),
            pltpu.VMEM((quads, side, chans, width), jnp.float32),
            pltpu.VMEM((quads, extra, chans, width), jnp.float32),
            pltpu.VMEM((quads, extra, chans, width), jnp.float32),
            pltpu.VMEM((channels + chans, 128), jnp.float32),
            pltpu.VMEM((128, channels), jnp.float32),
            pltpu.VMEM((taps, chans, width), jnp.float32),
        ],
        compiler_params=large,
        name="convs",
    )(sent, *params[:4])
    zonal = zonal[:, :share, :cells]
    returned = lax.all_to_all(zonal, ("face", "sub"), split_axis=0, concat_axis=0, tiled=True)

    output = pl.pallas_call(
        mlp_kernel,
        out_shape=jax.ShapeDtypeStruct(local.shape, jnp.bfloat16),
        in_specs=[vmem] * 6,
        out_specs=hbm,
        scratch_shapes=[
            pltpu.VMEM((rows, faces, side, channels), jnp.bfloat16),
            pltpu.SemaphoreType.DMA((rows,)),
        ],
        compiler_params=small,
        name="mlp",
    )(returned.reshape(channels, cells), local, *params[4:], w_in, w_out)
    return output.reshape(field.shape)


def solution(mesh):
    in_specs = (P(None, "face", "sub", None, None), P(), P(), P(), P(), P(), P(), P(), P())
    out_specs = P(None, "face", "sub", None, None)
    return jax.shard_map(shards, mesh=mesh, in_specs=in_specs, out_specs=out_specs, check_vma=False)
```

```python
import functools

import jax
import jax.numpy as jnp
from jax import lax
from jax.experimental import pallas as pl
from jax.experimental.pallas import tpu as pltpu
from jax.sharding import PartitionSpec as P

TAPS = 7
DILATION = 4
REACH = DILATION * (TAPS // 2)
EPSILON = 1e-06


def fold(count, body, carry, unroll):
    if unroll:
        for i in range(count):
            carry = body(i, carry)
        return carry
    return lax.fori_loop(0, count, body, carry)


def wrap(value, size):
    if isinstance(value, int):
        return value % size
    return lax.rem(value + size, size)


def shift_lanes(values, shift):
    width = values.shape[-1]
    if isinstance(shift, int):
        shift %= width
        if shift == 0:
            return values
    return pltpu.roll(values, shift, values.ndim - 1)


def piece_at(block, slot, faces=3):
    group, at = divmod(block, faces)
    first = group * (faces + 1)
    if slot < faces:
        return faces - 1 - slot, first + at
    return faces - 1 - at, first + faces


def conv_kernel(
    quads, subs, side, rows, share, axes, x_ref, dw_ref, dw_bias_ref, zonal_ref, zonal_bias_ref, o_ref,
    e_ref, m_ref, ahead_ref, behind_ref, columns, table, w_ref
):
    width = quads * side
    chans = x_ref.shape[1]
    unroll = width <= 128
    lane = lax.broadcasted_iota(jnp.int32, (chans, width), 1)
    blocks = 3 * rows // quads

    def load(source):
        return [
            x_ref[source, :, b * width : (b + 1) * width].astype(jnp.float32)
            for b in range(blocks)
        ]

    def plain_row(held, held_before, sub, local):
        group, at = divmod(local, 4)
        y = sub * rows + local
        first = 3 * group
        if at < 3:
            row = jnp.where(lane < side, held_before[first + at], held[first + at])
            return shift_lanes(row, y)
        south = shift_lanes(held_before[first], wrap(y - 3 * side, width))
        middle = shift_lanes(held[first + 1], wrap(y - 2 * side, width))
        north = shift_lanes(held[first + 2], wrap(y - side, width))
        return jnp.where(lane < y + side, south, jnp.where(lane < y + 2 * side, middle, north))

    last_held = [load(q * subs + subs - 1) for q in range(quads)]
    first_held = [load(q * subs) for q in range(quads)]
    beyond_right, beyond_left = [], []
    for q in range(quads):
        low = plain_row(last_held[q], last_held[q - 1], subs - 1, rows - 1)
        top = plain_row(first_held[q], first_held[q - 1], 0, 0)
        beyond_right.append(shift_lanes(low, 1))
        beyond_left.append(shift_lanes(top, width - 1))

    def build(sub, diagonals):
        diagonals = list(diagonals)
        held = [load(q * subs + sub) for q in range(quads)]
        for q in range(quads):
            for local in range(rows):
                y = sub * rows + local
                row = plain_row(held[q], held[q - 1], sub, local)
                diagonals[2 * q] = jnp.where(lane < y, diagonals[2 * q], row)
                diagonals[2 * q + 1] = jnp.where(
                    lane < y + 3 * side - 1, diagonals[2 * q + 1], row
                )
                row = jnp.where(lane < y + 3 * side, row, beyond_right[(q + 1) % quads])
                row = jnp.where(lane == wrap(y - 1, width), beyond_left[q - 1], row) if not isinstance(y, int) or y == 0 else jnp.where(lane < y, beyond_left[q - 1], row)
                e_ref[q, side - y] = row
        return tuple(diagonals)

    blank = jnp.zeros((chans, width), jnp.float32)
    diagonals = fold(subs, build, (blank,) * (2 * quads), unroll)
    for q in range(quads):
        after = (q + 1) % quads
        before = (q - 1) % quads
        e_ref[q, 0] = jnp.where(
            lane < 3 * side, e_ref[before, side], shift_lanes(diagonals[2 * before + 1], 1)
        )
        e_ref[q, side + 1] = jnp.where(
            (lane >= side - 1) & (lane < 3 * side - 1),
            e_ref[after, 1],
            shift_lanes(diagonals[2 * after], width - 1),
        )

    lay_out(share, axes, (dw_ref, dw_bias_ref, zonal_ref, zonal_bias_ref), columns, table, w_ref)

    def depthwise(q, u, first=False, last=False):
        below, here, above = e_ref[q, u], e_ref[q, u + 1], e_ref[q, u + 2]
        up_left = w_ref[0] * shift_lanes(above, 2)
        up_right = w_ref[2] * above
        down_left = w_ref[6] * below
        down_right = w_ref[8] * shift_lanes(below, width - 2)
        for k in range(3):
            if first:
                down_left = jnp.where(lane == side - 1 + k * side, 0.0, down_left)
                down_right = jnp.where(lane == 2 * side - 2 + k * side, 0.0, down_right)
            if last:
                up_left = jnp.where(lane == k * side, 0.0, up_left)
                up_right = jnp.where(lane == side - 1 + k * side, 0.0, up_right)
        total = w_ref[9] + w_ref[4] * here
        total = total + (up_right + down_left)
        total = total + (w_ref[1] * shift_lanes(above, 1) + w_ref[3] * shift_lanes(here, 1))
        total = total + (w_ref[5] * shift_lanes(here, width - 1) + w_ref[7] * shift_lanes(below, width - 1))
        total = total + (up_left + down_right)
        m_ref[q, u] = total.astype(jnp.bfloat16).astype(jnp.float32)

    for q in range(quads):
        depthwise(q, 0, first=True)

        def inner(u, carry, q=q):
            depthwise(q, u + 1)
            return carry

        fold(side - 2, inner, 0, unroll)
        depthwise(q, side - 1, last=True)

    north_cap, south_cap = lane >= 3 * side, lane < side - 1
    northern = lane >= 2 * side
    arc = jnp.where(north_cap, width - 1 - lane, jnp.where(south_cap, lane + 1, side))
    equator = jnp.logical_not(north_cap | south_cap)
    steps = []
    step = 1
    while step < side:
        steps.append(step)
        step *= 2
    has_step = {step: (arc & step) != 0 for step in steps}
    kept = {}

    def merged(j, d, tail):
        key = (j, d, tail)
        if unroll and key in kept:
            return kept[key]
        forth, back = m_ref[j, d], m_ref[wrap(quads - j, quads), side - 1 - d]
        line = jnp.where(northern, back, forth) if tail else jnp.where(northern, forth, back)
        if unroll:
            kept[key] = line
        return line

    def sheared(inputs):
        seen = {}

        def line(level, t):
            if level == len(steps):
                return inputs.get(t)
            if (level, t) not in seen:
                step = steps[level]
                still, moved = line(level + 1, t), line(level + 1, t - step)
                if still is not None and moved is not None:
                    moved = jnp.where(has_step[step], moved, still)
                seen[level, t] = still if moved is None else moved
            return seen[level, t]

        return lambda t: line(0, t)

    def extend(j, carry):
        back = wrap(quads - j, quads)
        forth_strip, back_strip = wrap(j - 1, quads), wrap(quads + 1 - j, quads)
        heads, tails = {}, {}
        for d in range(REACH):
            line = merged(j, d, False)
            for a in range(1, min(d + 1, REACH)):
                line = jnp.where(arc == a, merged(wrap(j + d // a, quads), d % a, False), line)
            heads[d] = line
        for d in range(1, side):
            tails[d] = merged(j, d, True)
        for d in range(side, side + REACH - 1):
            line = None
            for a in range(1, side + REACH - d):
                place = d - side + a
                moved = merged(wrap(j + place // a, quads), side - a + place % a, True)
                line = moved if line is None else jnp.where(arc == a, moved, line)
            tails[d] = line
        head, tail = sheared(heads), sheared(tails)
        for t in range(DILATION, side + REACH):
            line = head(t)
            if t < side:
                ahead = jnp.where(lane >= width - 1 - t, line, m_ref[forth_strip, t])
                behind = jnp.where(lane < t, line, m_ref[back_strip, side - 1 - t])
            else:
                end = tail(t)
                ahead = jnp.where(south_cap, end, end if line is None else line)
                behind = jnp.where(north_cap, end, end if line is None else line)
                ahead = jnp.where(equator, m_ref[j, t - side], ahead)
                behind = jnp.where(equator, m_ref[back, 2 * side - 1 - t], behind)
            ahead_ref[forth_strip, t - DILATION] = ahead
            behind_ref[back_strip, t - DILATION] = behind
        return carry

    fold(quads, extend, 0, unroll)

    half = TAPS // 2

    def zonal(q, u):
        total = w_ref[17] + w_ref[10 + half] * m_ref[q, u]
        for k in range(1, half + 1):
            pair = w_ref[10 + half + k] * ahead_ref[q, u + DILATION * (k - 1)]
            pair = pair + w_ref[10 + half - k] * behind_ref[q, side - 1 - u + DILATION * (k - 1)]
            total = total + pair
        return total

    def spread(sub, carry):
        seen = {}

        def row(q, local):
            q %= quads
            if (q, local) not in seen:
                seen[q, local] = zonal(q, side - 1 - sub * rows - local)
            return seen[q, local]

        for group in range(rows // 4):
            first = 4 * group
            y = sub * rows + first
            aligned = [
                [shift_lanes(row(q, first + at), wrap(width - y - at, width)) for q in range(quads)]
                for at in range(3)
            ]
            for q in range(quads):
                for at in range(3):
                    rest = row(q + 1 if at == 0 else q, first + 3)
                    rest = shift_lanes(rest, wrap((3 - at) * side - y - 3 + width, width))
                    block = jnp.where(
                        lane < side,
                        aligned[at][(q + 1) % quads],
                        jnp.where(lane < 3 * side, aligned[at][q], rest),
                    )
                    b = 3 * group + at
                    o_ref[q * subs + sub, :, b * width : (b + 1) * width] = block.astype(
                        jnp.bfloat16
                    )
        return carry

    fold(subs, spread, 0, unroll)


def lay_out(share, axes, params, columns, table, w_ref):
    first = 0
    for source in params:
        table[first : first + source.shape[0], :] = source[...]
        first += source.shape[0]
    columns[0 : table.shape[1], :] = table[...].T
    device = lax.axis_index(axes[0]) * lax.axis_size(axes[1]) + lax.axis_index(axes[1])
    start = device * share
    if share % 8 == 0:
        start = pl.multiple_of(start, 8)
    mine = columns[pl.ds(start, w_ref.shape[1]), :]
    for k in range(w_ref.shape[0]):
        w_ref[k] = jnp.broadcast_to(mine[:, k : k + 1], w_ref.shape[1:])


def pack_kernel(x_hbm, *refs):
    params, o_ref, held, x_vmem, x_sems, sems = refs[:6], refs[6], refs[7:13], refs[13], refs[14], refs[15]
    rows, _, side, channels = x_vmem.shape
    order = [at for at in range(rows) if at % 4 == 3] + [at for at in range(rows) if at % 4 != 3]
    loads = [
        pltpu.make_async_copy(x_hbm.at[:, at], x_vmem.at[at], x_sems.at[at]) for at in order
    ]
    small = [
        pltpu.make_async_copy(source, target, sems.at[i])
        for i, (source, target) in enumerate(zip(params, held, strict=True))
    ]
    for copy in small + loads:
        copy.start()
    for copy in loads:
        copy.wait()
    width = 4 * side
    for block in range(3 * rows // 4):
        pieces = [x_vmem[local, face] for face, local in (piece_at(block, k) for k in range(4))]
        o_ref[:, block * width : (block + 1) * width] = jnp.concatenate(pieces, 0).T
    for copy in small:
        copy.wait()


def mlp_kernel(z_ref, x_ref, gain_ref, scale_ref, w_in_ref, w_out_ref, o_hbm, o_vmem, sems):
    parts, slots, side, _ = o_vmem.shape
    width = slots * side
    gain, scale = gain_ref[...], scale_ref[...]
    stores = []
    for i in range(parts):
        values = z_ref[:, i * width : (i + 1) * width].astype(jnp.float32)
        mean = jnp.mean(values, 0, keepdims=True)
        values = values - mean
        spread = jnp.mean(jnp.square(values), 0, keepdims=True)
        values = values * lax.rsqrt(spread + EPSILON)
        normed = (values.T * gain).astype(jnp.bfloat16)
        inner = jnp.dot(normed, w_in_ref[...], preferred_element_type=jnp.float32)
        hidden = (0.5 * inner * (1.0 + lax.erf(inner * 0.5**0.5))).astype(jnp.bfloat16)
        branch = jnp.dot(hidden, w_out_ref[...], preferred_element_type=jnp.float32)
        for k in range(slots):
            face, local = piece_at(i, k)
            source = x_ref[face, local].astype(jnp.float32)
            place = face if k < slots - 1 else k
            o_vmem[i, place] = (source + scale * branch[k * side : (k + 1) * side]).astype(jnp.bfloat16)
        line = piece_at(i, 0)[1]
        face, local = piece_at(i, slots - 1)
        for at, (source, target) in enumerate(
            (
                (o_vmem.at[i, pl.ds(0, slots - 1)], o_hbm.at[:, line]),
                (o_vmem.at[i, slots - 1], o_hbm.at[face, local]),
            )
        ):
            store = pltpu.make_async_copy(source, target, sems.at[2 * i + at])
            store.start()
            stores.append(store)
    for store in stores:
        store.wait()


def shards(
    field, dw_kernel, dw_bias, zonal_kernel, zonal_bias, norm_gain, w_in, w_out, layer_scale
):
    faces, _, rows, side, channels = field.shape
    quads, subs = lax.axis_size("face"), lax.axis_size("sub")
    devices = quads * subs
    share = channels // devices
    cells = faces * rows * side
    width = quads * side
    lanes = -(-cells // width) * width
    chans = -(-share // 8) * 8
    vmem = pl.BlockSpec(memory_space=pltpu.VMEM)
    small = pltpu.CompilerParams(vmem_limit_bytes=2**20 + 24 * cells * channels)
    field_bytes = 4 * devices * chans * lanes
    large = pltpu.CompilerParams(vmem_limit_bytes=2**20 + 9 * field_bytes)

    local = field.reshape(faces, rows, side, channels)
    hbm = pl.BlockSpec(memory_space=pltpu.HBM)
    params = (
        dw_kernel, dw_bias[None], zonal_kernel, zonal_bias[None], norm_gain[None], layer_scale[None]
    )
    taps = sum(p.shape[0] for p in params[:4])
    packed, *params = pl.pallas_call(
        pack_kernel,
        out_shape=(
            jax.ShapeDtypeStruct((channels, cells), jnp.bfloat16),
            *(jax.ShapeDtypeStruct(p.shape, jnp.float32) for p in params),
        ),
        in_specs=[hbm] * 7,
        out_specs=(vmem,) * 7,
        scratch_shapes=[
            pltpu.VMEM((rows, faces, side, channels), jnp.bfloat16),
            pltpu.SemaphoreType.DMA((rows,)),
            pltpu.SemaphoreType.DMA((len(params),)),
        ],
        compiler_params=small,
        name="pack",
    )(*(pltpu.with_memory_space_constraint(array, pltpu.HBM) for array in (local, *params)))
    sent = lax.all_to_all(
        packed.reshape(devices, share, cells), ("face", "sub"), split_axis=0, concat_axis=0, tiled=True
    )
    sent = jnp.pad(sent, ((0, 0), (0, chans - share), (0, lanes - cells)))

    extra = side + REACH - DILATION
    zonal = pl.pallas_call(
        functools.partial(conv_kernel, quads, subs, side, rows, share, ("face", "sub")),
        out_shape=jax.ShapeDtypeStruct((devices, chans, lanes), jnp.bfloat16),
        in_specs=[vmem] * 5,
        out_specs=vmem,
        scratch_shapes=[
            pltpu.VMEM((quads, side + 2, chans, width), jnp.float32),
            pltpu.VMEM((quads, side, chans, width), jnp.float32),
            pltpu.VMEM((quads, extra, chans, width), jnp.float32),
            pltpu.VMEM((quads, extra, chans, width), jnp.float32),
            pltpu.VMEM((channels + chans, 128), jnp.float32),
            pltpu.VMEM((128, channels), jnp.float32),
            pltpu.VMEM((taps, chans, width), jnp.float32),
        ],
        compiler_params=large,
        name="convs",
    )(sent, *params[:4])
    zonal = zonal[:, :share, :cells]
    returned = lax.all_to_all(zonal, ("face", "sub"), split_axis=0, concat_axis=0, tiled=True)

    output = pl.pallas_call(
        mlp_kernel,
        out_shape=jax.ShapeDtypeStruct(local.shape, jnp.bfloat16),
        in_specs=[vmem] * 6,
        out_specs=hbm,
        scratch_shapes=[
            pltpu.VMEM((cells // width, quads, side, channels), jnp.bfloat16),
            pltpu.SemaphoreType.DMA((2 * cells // width,)),
        ],
        compiler_params=small,
        name="mlp",
    )(returned.reshape(channels, cells), local, *params[4:], w_in, w_out)
    return output.reshape(field.shape)


def solution(mesh):
    in_specs = (P(None, "face", "sub", None, None), P(), P(), P(), P(), P(), P(), P(), P())
    out_specs = P(None, "face", "sub", None, None)
    return jax.shard_map(shards, mesh=mesh, in_specs=in_specs, out_specs=out_specs, check_vma=False)
```

```python
import functools

import jax
import jax.numpy as jnp
from jax import lax
from jax.experimental import pallas as pl
from jax.experimental.pallas import tpu as pltpu
from jax.sharding import PartitionSpec as P

TAPS = 7
DILATION = 4
REACH = DILATION * (TAPS // 2)
EPSILON = 1e-06


def fold(count, body, carry, unroll):
    if unroll:
        for i in range(count):
            carry = body(i, carry)
        return carry
    return lax.fori_loop(0, count, body, carry)


def wrap(value, size):
    if isinstance(value, int):
        return value % size
    return lax.rem(value + size, size)


def shift_lanes(values, shift):
    width = values.shape[-1]
    if isinstance(shift, int):
        shift %= width
        if shift == 0:
            return values
    return pltpu.roll(values, shift, values.ndim - 1)


def piece_at(block, slot, faces=3):
    group, at = divmod(block, faces)
    first = group * (faces + 1)
    if slot < faces:
        return faces - 1 - slot, first + at
    return faces - 1 - at, first + faces


def conv_kernel(
    quads, subs, side, rows, share, axes, x_ref, dw_ref, dw_bias_ref, zonal_ref, zonal_bias_ref, o_ref,
    e_ref, m_ref, ahead_ref, behind_ref, columns, table, w_ref
):
    width = quads * side
    chans = x_ref.shape[1]
    unroll = width <= 128
    lane = lax.broadcasted_iota(jnp.int32, (chans, width), 1)
    blocks = 3 * rows // quads

    def load(source):
        return [
            x_ref[source, :, b * width : (b + 1) * width].astype(jnp.float32)
            for b in range(blocks)
        ]

    def plain_row(held, held_before, sub, local):
        group, at = divmod(local, 4)
        y = sub * rows + local
        first = 3 * group
        if at < 3:
            row = jnp.where(lane < side, held_before[first + at], held[first + at])
            return shift_lanes(row, y)
        south = shift_lanes(held_before[first], wrap(y - 3 * side, width))
        middle = shift_lanes(held[first + 1], wrap(y - 2 * side, width))
        north = shift_lanes(held[first + 2], wrap(y - side, width))
        return jnp.where(lane < y + side, south, jnp.where(lane < y + 2 * side, middle, north))

    last_held = [load(q * subs + subs - 1) for q in range(quads)]
    first_held = [load(q * subs) for q in range(quads)]
    beyond_right, beyond_left = [], []
    for q in range(quads):
        low = plain_row(last_held[q], last_held[q - 1], subs - 1, rows - 1)
        top = plain_row(first_held[q], first_held[q - 1], 0, 0)
        beyond_right.append(shift_lanes(low, 1))
        beyond_left.append(shift_lanes(top, width - 1))

    def build(sub, diagonals):
        diagonals = list(diagonals)
        held = [load(q * subs + sub) for q in range(quads)]
        for q in range(quads):
            for local in range(rows):
                y = sub * rows + local
                row = plain_row(held[q], held[q - 1], sub, local)
                diagonals[2 * q] = jnp.where(lane < y, diagonals[2 * q], row)
                diagonals[2 * q + 1] = jnp.where(
                    lane < y + 3 * side - 1, diagonals[2 * q + 1], row
                )
                row = jnp.where(lane < y + 3 * side, row, beyond_right[(q + 1) % quads])
                row = jnp.where(lane == wrap(y - 1, width), beyond_left[q - 1], row) if not isinstance(y, int) or y == 0 else jnp.where(lane < y, beyond_left[q - 1], row)
                e_ref[q, side - y] = row
        return tuple(diagonals)

    blank = jnp.zeros((chans, width), jnp.float32)
    diagonals = fold(subs, build, (blank,) * (2 * quads), unroll)
    for q in range(quads):
        after = (q + 1) % quads
        before = (q - 1) % quads
        e_ref[q, 0] = jnp.where(
            lane < 3 * side, e_ref[before, side], shift_lanes(diagonals[2 * before + 1], 1)
        )
        e_ref[q, side + 1] = jnp.where(
            (lane >= side - 1) & (lane < 3 * side - 1),
            e_ref[after, 1],
            shift_lanes(diagonals[2 * after], width - 1),
        )

    lay_out(share, axes, (dw_ref, dw_bias_ref, zonal_ref, zonal_bias_ref), columns, table, w_ref)

    def depthwise(q, u, first=False, last=False):
        below, here, above = e_ref[q, u], e_ref[q, u + 1], e_ref[q, u + 2]
        up_left = w_ref[0] * shift_lanes(above, 2)
        up_right = w_ref[2] * above
        down_left = w_ref[6] * below
        down_right = w_ref[8] * shift_lanes(below, width - 2)
        for k in range(3):
            if first:
                down_left = jnp.where(lane == side - 1 + k * side, 0.0, down_left)
                down_right = jnp.where(lane == 2 * side - 2 + k * side, 0.0, down_right)
            if last:
                up_left = jnp.where(lane == k * side, 0.0, up_left)
                up_right = jnp.where(lane == side - 1 + k * side, 0.0, up_right)
        total = w_ref[9] + w_ref[4] * here
        total = total + (up_right + down_left)
        total = total + (w_ref[1] * shift_lanes(above, 1) + w_ref[3] * shift_lanes(here, 1))
        total = total + (w_ref[5] * shift_lanes(here, width - 1) + w_ref[7] * shift_lanes(below, width - 1))
        total = total + (up_left + down_right)
        m_ref[q, u] = total.astype(jnp.bfloat16).astype(jnp.float32)

    for q in range(quads):
        depthwise(q, 0, first=True)

        def inner(u, carry, q=q):
            depthwise(q, u + 1)
            return carry

        fold(side - 2, inner, 0, unroll)
        depthwise(q, side - 1, last=True)

    north_cap, south_cap = lane >= 3 * side, lane < side - 1
    northern = lane >= 2 * side
    arc = jnp.where(north_cap, width - 1 - lane, jnp.where(south_cap, lane + 1, side))
    equator = jnp.logical_not(north_cap | south_cap)
    steps = []
    step = 1
    while step < side:
        steps.append(step)
        step *= 2
    has_step = {step: (arc & step) != 0 for step in steps}
    kept = {}

    def merged(j, d, tail):
        key = (j, d, tail)
        if unroll and key in kept:
            return kept[key]
        forth, back = m_ref[j, d], m_ref[wrap(quads - j, quads), side - 1 - d]
        line = jnp.where(northern, back, forth) if tail else jnp.where(northern, forth, back)
        if unroll:
            kept[key] = line
        return line

    def sheared(inputs):
        seen = {}

        def line(level, t):
            if level == len(steps):
                return inputs.get(t)
            if (level, t) not in seen:
                step = steps[level]
                still, moved = line(level + 1, t), line(level + 1, t - step)
                if still is not None and moved is not None:
                    moved = jnp.where(has_step[step], moved, still)
                seen[level, t] = still if moved is None else moved
            return seen[level, t]

        return lambda t: line(0, t)

    def extend(j, carry):
        back = wrap(quads - j, quads)
        forth_strip, back_strip = wrap(j - 1, quads), wrap(quads + 1 - j, quads)
        heads, tails = {}, {}
        for d in range(REACH):
            line = merged(j, d, False)
            for a in range(1, min(d + 1, REACH)):
                line = jnp.where(arc == a, merged(wrap(j + d // a, quads), d % a, False), line)
            heads[d] = line
        for d in range(1, side):
            tails[d] = merged(j, d, True)
        for d in range(side, side + REACH - 1):
            line = None
            for a in range(1, side + REACH - d):
                place = d - side + a
                moved = merged(wrap(j + place // a, quads), side - a + place % a, True)
                line = moved if line is None else jnp.where(arc == a, moved, line)
            tails[d] = line
        head, tail = sheared(heads), sheared(tails)
        for t in range(DILATION, side + REACH):
            line = head(t)
            if t < side:
                ahead = jnp.where(lane >= width - 1 - t, line, m_ref[forth_strip, t])
                behind = jnp.where(lane < t, line, m_ref[back_strip, side - 1 - t])
            else:
                end = tail(t)
                ahead = jnp.where(south_cap, end, end if line is None else line)
                behind = jnp.where(north_cap, end, end if line is None else line)
                ahead = jnp.where(equator, m_ref[j, t - side], ahead)
                behind = jnp.where(equator, m_ref[back, 2 * side - 1 - t], behind)
            ahead_ref[forth_strip, t - DILATION] = ahead
            behind_ref[back_strip, t - DILATION] = behind
        return carry

    fold(quads, extend, 0, unroll)

    half = TAPS // 2

    def zonal(q, u):
        total = w_ref[17] + w_ref[10 + half] * m_ref[q, u]
        for k in range(1, half + 1):
            pair = w_ref[10 + half + k] * ahead_ref[q, u + DILATION * (k - 1)]
            pair = pair + w_ref[10 + half - k] * behind_ref[q, side - 1 - u + DILATION * (k - 1)]
            total = total + pair
        return total

    def spread(sub, carry):
        seen = {}

        def row(q, local):
            q %= quads
            if (q, local) not in seen:
                seen[q, local] = zonal(q, side - 1 - sub * rows - local)
            return seen[q, local]

        for group in range(rows // 4):
            first = 4 * group
            y = sub * rows + first
            aligned = [
                [shift_lanes(row(q, first + at), wrap(width - y - at, width)) for q in range(quads)]
                for at in range(3)
            ]
            for q in range(quads):
                for at in range(3):
                    rest = row(q + 1 if at == 0 else q, first + 3)
                    rest = shift_lanes(rest, wrap((3 - at) * side - y - 3 + width, width))
                    block = jnp.where(
                        lane < side,
                        aligned[at][(q + 1) % quads],
                        jnp.where(lane < 3 * side, aligned[at][q], rest),
                    )
                    b = 3 * group + at
                    o_ref[q * subs + sub, :, b * width : (b + 1) * width] = block.astype(
                        jnp.bfloat16
                    )
        return carry

    fold(subs, spread, 0, unroll)


def lay_out(share, axes, params, columns, table, w_ref):
    first = 0
    for source in params:
        table[first : first + source.shape[0], :] = source[...]
        first += source.shape[0]
    columns[0 : table.shape[1], :] = table[...].T
    device = lax.axis_index(axes[0]) * lax.axis_size(axes[1]) + lax.axis_index(axes[1])
    start = device * share
    if share % 8 == 0:
        start = pl.multiple_of(start, 8)
    mine = columns[pl.ds(start, w_ref.shape[1]), :]
    for k in range(w_ref.shape[0]):
        w_ref[k] = jnp.broadcast_to(mine[:, k : k + 1], w_ref.shape[1:])


def pack_kernel(x_hbm, *refs):
    params, o_ref, held, x_vmem, x_sems, sems = refs[:6], refs[6], refs[7:13], refs[13], refs[14], refs[15]
    rows, _, side, channels = x_vmem.shape
    order = [at for at in range(rows) if at % 4 == 3] + [at for at in range(rows) if at % 4 != 3]
    loads = [
        pltpu.make_async_copy(x_hbm.at[:, at], x_vmem.at[at], x_sems.at[at]) for at in order
    ]
    small = [
        pltpu.make_async_copy(source, target, sems.at[i])
        for i, (source, target) in enumerate(zip(params, held, strict=True))
    ]
    for copy in small + loads:
        copy.start()
    for copy in small + loads:
        copy.wait()
    width = 4 * side
    for block in range(3 * rows // 4):
        pieces = [x_vmem[local, face] for face, local in (piece_at(block, k) for k in range(4))]
        o_ref[:, block * width : (block + 1) * width] = jnp.concatenate(pieces, 0).T


def mlp_kernel(z_ref, x_ref, gain_ref, scale_ref, w_in_ref, w_out_ref, o_hbm, o_vmem, sems):
    parts, slots, side, _ = o_vmem.shape
    width = slots * side
    gain, scale = gain_ref[...], scale_ref[...]
    stores = []
    for i in range(parts):
        values = z_ref[:, i * width : (i + 1) * width].astype(jnp.float32)
        mean = jnp.mean(values, 0, keepdims=True)
        values = values - mean
        spread = jnp.mean(jnp.square(values), 0, keepdims=True)
        values = values * lax.rsqrt(spread + EPSILON)
        normed = (values.T * gain).astype(jnp.bfloat16)
        inner = jnp.dot(normed, w_in_ref[...], preferred_element_type=jnp.float32)
        half = 0.5 * inner
        hidden = (half + half * lax.erf(inner * 0.5**0.5)).astype(jnp.bfloat16)
        branch = jnp.dot(hidden, w_out_ref[...], preferred_element_type=jnp.float32)
        for k in range(slots):
            face, local = piece_at(i, k)
            source = x_ref[face, local].astype(jnp.float32)
            place = face if k < slots - 1 else k
            o_vmem[i, place] = (source + scale * branch[k * side : (k + 1) * side]).astype(jnp.bfloat16)
        line = piece_at(i, 0)[1]
        face, local = piece_at(i, slots - 1)
        for at, (source, target) in enumerate(
            (
                (o_vmem.at[i, pl.ds(0, slots - 1)], o_hbm.at[:, line]),
                (o_vmem.at[i, slots - 1], o_hbm.at[face, local]),
            )
        ):
            store = pltpu.make_async_copy(source, target, sems.at[2 * i + at])
            store.start()
            stores.append(store)
    for store in stores:
        store.wait()


def shards(
    field, dw_kernel, dw_bias, zonal_kernel, zonal_bias, norm_gain, w_in, w_out, layer_scale
):
    faces, _, rows, side, channels = field.shape
    quads, subs = lax.axis_size("face"), lax.axis_size("sub")
    devices = quads * subs
    share = channels // devices
    cells = faces * rows * side
    width = quads * side
    lanes = -(-cells // width) * width
    chans = -(-share // 8) * 8
    vmem = pl.BlockSpec(memory_space=pltpu.VMEM)
    small = pltpu.CompilerParams(vmem_limit_bytes=2**20 + 24 * cells * channels)
    field_bytes = 4 * devices * chans * lanes
    large = pltpu.CompilerParams(vmem_limit_bytes=2**20 + 9 * field_bytes)

    local = field.reshape(faces, rows, side, channels)
    hbm = pl.BlockSpec(memory_space=pltpu.HBM)
    params = (
        dw_kernel, dw_bias[None], zonal_kernel, zonal_bias[None], norm_gain[None], layer_scale[None]
    )
    taps = sum(p.shape[0] for p in params[:4])
    packed, *params = pl.pallas_call(
        pack_kernel,
        out_shape=(
            jax.ShapeDtypeStruct((channels, cells), jnp.bfloat16),
            *(jax.ShapeDtypeStruct(p.shape, jnp.float32) for p in params),
        ),
        in_specs=[hbm] * 7,
        out_specs=(vmem,) * 7,
        scratch_shapes=[
            pltpu.VMEM((rows, faces, side, channels), jnp.bfloat16),
            pltpu.SemaphoreType.DMA((rows,)),
            pltpu.SemaphoreType.DMA((len(params),)),
        ],
        compiler_params=small,
        name="pack",
    )(*(pltpu.with_memory_space_constraint(array, pltpu.HBM) for array in (local, *params)))
    sent = lax.all_to_all(
        packed.reshape(devices, share, cells), ("face", "sub"), split_axis=0, concat_axis=0, tiled=True
    )
    sent = jnp.pad(sent, ((0, 0), (0, chans - share), (0, lanes - cells)))

    extra = side + REACH - DILATION
    zonal = pl.pallas_call(
        functools.partial(conv_kernel, quads, subs, side, rows, share, ("face", "sub")),
        out_shape=jax.ShapeDtypeStruct((devices, chans, lanes), jnp.bfloat16),
        in_specs=[vmem] * 5,
        out_specs=vmem,
        scratch_shapes=[
            pltpu.VMEM((quads, side + 2, chans, width), jnp.float32),
            pltpu.VMEM((quads, side, chans, width), jnp.float32),
            pltpu.VMEM((quads, extra, chans, width), jnp.float32),
            pltpu.VMEM((quads, extra, chans, width), jnp.float32),
            pltpu.VMEM((channels + chans, 128), jnp.float32),
            pltpu.VMEM((128, channels), jnp.float32),
            pltpu.VMEM((taps, chans, width), jnp.float32),
        ],
        compiler_params=large,
        name="convs",
    )(sent, *params[:4])
    zonal = zonal[:, :share, :cells]
    returned = lax.all_to_all(zonal, ("face", "sub"), split_axis=0, concat_axis=0, tiled=True)

    output = pl.pallas_call(
        mlp_kernel,
        out_shape=jax.ShapeDtypeStruct(local.shape, jnp.bfloat16),
        in_specs=[vmem] * 6,
        out_specs=hbm,
        scratch_shapes=[
            pltpu.VMEM((cells // width, quads, side, channels), jnp.bfloat16),
            pltpu.SemaphoreType.DMA((2 * cells // width,)),
        ],
        compiler_params=small,
        name="mlp",
    )(returned.reshape(channels, cells), local, *params[4:], w_in, w_out)
    return output.reshape(field.shape)


def solution(mesh):
    in_specs = (P(None, "face", "sub", None, None), P(), P(), P(), P(), P(), P(), P(), P())
    out_specs = P(None, "face", "sub", None, None)
    return jax.shard_map(shards, mesh=mesh, in_specs=in_specs, out_specs=out_specs, check_vma=False)
```
